128 devices in a mesh: face: 4 (over x), tile: 32 (over y, z, core).
Axes of the slice: x: 4, y: 4, z: 4, core: 2. Of those that a mesh axis runs over, the one named last changes fastest.
Arguments:
- cells: bfloat16 [96, 768, 4096], P(None, 'face', 'tile'), may hold values from -6 to 6
- conv_in: bfloat16 [96, 864], replicated, may hold values from -0.21875 to 0.21875
- conv_out: bfloat16 [45, 864], replicated, may hold values from -0.21875 to 0.21875
- blend_cycle: int32 [512], P(('face', 'tile')), may hold values from 0 to 767, as said below
- blend_weight: float32 [512], P(('face', 'tile')), may hold values from 0 to 1
Outputs:
- regridded: bfloat16 [45, 512, 7200], P(None, ('face', 'tile'))
The draws below stay inside these ranges and needn't reach their ends.
Inputs may be any that keep to these rules, and one draw needn't show every extreme that they name: Latitude row j blends cycles of owner j // 4: blend_cycle[j] lies in (j // 4) * 6 to (j // 4) * 6 + 5, and equals the top of that range when j % 4 = 3.
All inputs are finite; a program needn't handle non-finite values.
Results may differ from the reference program's by a relative error of at most 0.009.
Values may be sent and summed in bfloat16 or wider, within the bound.
No kernel may reach another device: no remote copies, remote signals or barrier semaphores. Data moves between devices by JAX's collectives and lax.ppermute only.
A program may use at most 640 MiB of HBM per device.

```python
import math
import jax
import jax.numpy as jnp

C = 96
OUT = 45
MODES = 1024
LON = 7200
CYCLE_DEV = 6
LAT_DEV = 4
CYCLE = 4096
CYCLES = 768
LAT = 512


def draw_blend_cycle(key, part):
    key = jax.random.fold_in(key, 7)
    row_index = jnp.arange(LAT, dtype=jnp.int32)
    owner_index = row_index // LAT_DEV
    offsets = jax.random.randint(key, (LAT,), 0, CYCLE_DEV, dtype=jnp.int32)
    offsets = jnp.where(row_index % LAT_DEV == LAT_DEV - 1, CYCLE_DEV - 1, offsets)
    offsets = jnp.where(row_index == 0, 0, offsets)
    return (owner_index * CYCLE_DEV + offsets).astype(jnp.int32)


def block_scale(key, dims, pieces, smallest, high):
    gain, own = 1.0, jax.random.fold_in(key, 6)
    for axis_at, shards_of in pieces:
        draws = jnp.exp(jax.random.uniform(jax.random.fold_in(own, axis_at), (shards_of,), jnp.float32, smallest / len(pieces), high / len(pieces)))
        gain = gain * jnp.repeat(draws, dims[axis_at] // shards_of).reshape([-1 if axis == axis_at else 1 for axis in range(len(dims))])
    return gain


def gaussian(rng, dims, spread, bound, pieces=(), kind=jnp.bfloat16):
    result = jax.random.normal(rng, dims, jnp.float32) * spread
    if len(pieces) > 0:
        result = block_scale(rng, dims, pieces, -0.22, 0.18) * result
    return jnp.clip(result, min=-bound, max=bound).astype(kind)


def setup_inputs(seed: int = 0) -> dict:
    splits = jax.random.split(jax.random.key(seed), 6)
    cells = gaussian(splits[0], (C, CYCLES, CYCLE), 1.0, 6.0, ((1, 4), (2, 32)))
    conv_in = gaussian(splits[1], (C, 9 * C), (9 * C) ** -0.5, 0.21875)
    conv_out = gaussian(splits[2], (OUT, 9 * C), (9 * C) ** -0.5, 0.21875)
    blend_cycle = draw_blend_cycle(jax.random.fold_in(splits[5], 71), 0)
    blend_weight = jnp.clip(1.0 * jax.random.uniform(splits[4], (LAT,), jnp.float32) ** block_scale(splits[4], (LAT,), ((0, 128),), -0.2, 0.2), 0.0, 1.0)
    return dict(cells=cells, conv_in=conv_in, conv_out=conv_out, blend_cycle=blend_cycle, blend_weight=blend_weight)


def forward_basis(first_pixel, pixel_count, cycle_len, mode_count):
    pixel_index = jnp.arange(pixel_count, dtype=jnp.int32) + first_pixel
    mode_index = jnp.arange(mode_count, dtype=jnp.int32)
    angles = ((pixel_index[:, None] * mode_index[None, :]) % cycle_len).astype(jnp.float32) * (2.0 * math.pi / cycle_len)
    return jnp.concatenate([jnp.cos(angles), jnp.sin(angles)], axis=1).astype(jnp.bfloat16)


def inverse_basis(mode_count, lon_count, cycle_len):
    mode_index = jnp.arange(mode_count, dtype=jnp.int32)
    lon_index = jnp.arange(lon_count, dtype=jnp.int32)
    angles = ((mode_index[:, None] * lon_index[None, :]) % lon_count).astype(jnp.float32) * (2.0 * math.pi / lon_count)
    weighting = jnp.where(mode_index == 0, 1.0, 2.0).astype(jnp.float32) / cycle_len
    return jnp.concatenate([weighting[:, None] * jnp.cos(angles), weighting[:, None] * jnp.sin(angles)], axis=0).astype(jnp.bfloat16)


def convolve(grid_field, weight):
    channels, row_count, col_count = grid_field.shape
    padded = jnp.pad(grid_field, ((0, 0), (1, 1), (0, 0)))
    padded = jnp.concatenate([padded[:, :, -1:], padded, padded[:, :, :1]], axis=2)
    total = jnp.zeros((weight.shape[0], row_count * col_count), jnp.float32)
    for row_step in range(3):
        for col_step in range(3):
            tap_index = row_step * 3 + col_step
            piece = padded[:, row_step:row_step + row_count, col_step:col_step + col_count].reshape(channels, row_count * col_count)
            total = total + jnp.dot(weight[:, tap_index * channels:(tap_index + 1) * channels], piece, preferred_element_type=jnp.float32)
    return total.reshape(weight.shape[0], row_count, col_count)


def reference(cells, conv_in, conv_out, blend_cycle, blend_weight):
    hidden = jax.nn.silu(convolve(cells, conv_in)).astype(jnp.bfloat16)
    fields = convolve(hidden, conv_out).astype(jnp.bfloat16)
    spectra = jnp.dot(fields.reshape(OUT * CYCLES, CYCLE), forward_basis(0, CYCLE, CYCLE, MODES), preferred_element_type=jnp.float32).reshape(OUT, CYCLES, 2 * MODES)
    padded = jnp.concatenate([spectra, jnp.zeros((OUT, 1, 2 * MODES), jnp.float32)], axis=1)
    lower_cycle = padded[:, blend_cycle.astype(jnp.int32), :]
    upper_cycle = padded[:, (blend_cycle + 1).astype(jnp.int32), :]
    weight_column = blend_weight[None, :, None]
    blended = ((1.0 - weight_column) * lower_cycle + weight_column * upper_cycle).astype(jnp.bfloat16)
    regridded = jnp.dot(blended.reshape(OUT * LAT, 2 * MODES), inverse_basis(MODES, LON, CYCLE), preferred_element_type=jnp.float32)
    return regridded.reshape(OUT, LAT, LON).astype(jnp.bfloat16)
```

```python
import jax
import jax.numpy as jnp
import numpy as np
from jax import lax
from jax.sharding import PartitionSpec as P
from jax.experimental import pallas as pl
from jax.experimental.pallas import tpu as pltpu
BF, F32 = jnp.bfloat16, jnp.float32
VLIM = 60 * 1024 * 1024

def regroup_kernel(x_ref, o_ref, s_ref):
    c, r, p = x_ref.shape
    s_ref[...] = x_ref[...].astype(F32).reshape(c * r, p)
    for i in range(r):
        o_ref[i] = s_ref[pl.ds(i, c, stride=r), :].astype(BF)

def regroup(x, rb=16):
    c, r, p = x.shape
    return pl.pallas_call(
        regroup_kernel,
        out_shape=jax.ShapeDtypeStruct((r, c, p), BF),
        grid=(r // rb,),
        in_specs=[pl.BlockSpec((c, rb, p), lambda i: (0, i, 0))],
        out_specs=pl.BlockSpec((rb, c, p), lambda i: (i, 0, 0)),
        scratch_shapes=[pltpu.VMEM((c * rb, p), F32)],
        compiler_params=pltpu.CompilerParams(vmem_limit_bytes=VLIM),
    )(x)

def silu(v):
    return v / (1.0 + jnp.exp(-v))

def with_sides(mid, left, right, i):
    lane = lax.broadcasted_iota(jnp.int32, mid.shape, 1)
    t, l = i // 128, i % 128
    el = pltpu.roll(left[t], (128 - l) % 128, axis=1)
    er = pltpu.roll(right[t], 127 - l, axis=1)
    before = jnp.where(lane == 0, el, pltpu.roll(mid, 1, axis=1))
    after = jnp.where(lane == 127, er, pltpu.roll(mid, 127, axis=1))
    return before.astype(BF), after.astype(BF)

def conv_kernel(face_ref, w1_ref, w2_ref, x_ref, up_ref, dn_ref, l_ref, s_ref, r_ref, f_ref,
                x3, h3, xl, xr, hl, hr):
    C = 96
    face = face_ref[0]
    R = x_ref.shape[0]
    w1 = w1_ref[...]
    w2 = w2_ref[...]
    for t in range(2):
        xl[t] = l_ref[1, :, t * 128:(t + 1) * 128].astype(F32)
        xr[t] = r_ref[0, :, t * 128:(t + 1) * 128].astype(F32)
    row = lax.broadcasted_iota(jnp.int32, (C, 256), 1) - 1
    lo = jnp.where(face == 0, 0, -1)
    hi = jnp.where(face == 3, R, R + 2)
    for cols, dst in (((l_ref[0], l_ref[1], s_ref[0]), hl), ((s_ref[3], r_ref[0], r_ref[1]), hr)):
        stack = []
        for a in range(3):
            for c in cols:
                c = c.astype(F32)
                stack.append((c if a == 0 else pltpu.roll(c, 256 - a, axis=1)).astype(BF))
        v = silu(jnp.dot(w1, jnp.concatenate(stack, axis=0), preferred_element_type=F32))
        v = jnp.where((row >= lo) & (row < hi), v, 0.0)
        dst[0] = v[:, :128]
        dst[1] = v[:, 128:]

    def put_x(i, mid):
        b, a = with_sides(mid.astype(F32), xl, xr, i)
        x3[i, 0:C] = b
        x3[i, C:2 * C] = mid
        x3[i, 2 * C:3 * C] = a

    for i in range(2):
        put_x(i, up_ref[i])
    for i in range(3):
        put_x(R + 2 + i, dn_ref[i])

    @pl.loop(0, R, step=4)
    def _(r):
        for u in range(4):
            put_x(r + u + 2, x_ref[r + u])

    def hid(k, n):
        cols = [x3[pl.ds(k + u, 3)].reshape(9 * C, 128) for u in range(n)]
        v = jnp.dot(w1, jnp.concatenate(cols, axis=1), preferred_element_type=F32)
        v = silu(v)
        for u in range(n):
            rr = k + u - 1
            ok = (rr >= lo) & (rr < hi)
            vu = jnp.where(ok, v[:, u * 128:(u + 1) * 128], 0.0)
            b, a = with_sides(vu, hl, hr, k + u)
            h3[k + u, 0:C] = b
            h3[k + u, C:2 * C] = vu.astype(BF)
            h3[k + u, 2 * C:3 * C] = a

    @pl.loop(0, R + 2, step=2)
    def _(k):
        hid(k, 2)
    hid(R + 2, 1)

    def fld(r, n):
        cols = [h3[pl.ds(r + u, 3)].reshape(9 * C, 128) for u in range(n)]
        v = jnp.dot(w2, jnp.concatenate(cols, axis=1), preferred_element_type=F32)
        for u in range(n):
            f_ref[r + u] = v[:, u * 128:(u + 1) * 128].astype(BF)

    @pl.loop(0, R, step=2)
    def _(r):
        fld(r, 2)
    v = jnp.dot(w2, h3[pl.ds(R, 3)].reshape(9 * C, 128), preferred_element_type=F32)
    f_ref[R] = jnp.where(face == 3, 0.0, v).astype(BF)

def conv(face, w1, w2, x, up, dn, l, s, r):
    R = x.shape[0]
    V = pl.BlockSpec(memory_space=pltpu.VMEM)
    return pl.pallas_call(
        conv_kernel,
        out_shape=jax.ShapeDtypeStruct((R + 1, 48, 128), BF),
        in_specs=[pl.BlockSpec(memory_space=pltpu.SMEM)] + [V] * 8,
        out_specs=V,
        scratch_shapes=[pltpu.VMEM((R + 5, 288, 128), BF), pltpu.VMEM((R + 3, 288, 128), BF)]
        + [pltpu.VMEM((2, 96, 128), F32)] * 4,
        compiler_params=pltpu.CompilerParams(vmem_limit_bytes=VLIM),
    )(face, w1, w2, x, up, dn, l, s, r)

def blend_kernel(p_ref, f_ref, o_ref, s_ref):
    D = o_ref.shape[0]
    @pl.loop(0, D)
    def _(d):
        for j in range(4):
            c = d * 6 + p_ref[d, j].astype(jnp.int32)
            w = p_ref[d, 4 + j]
            v = (1.0 - w) * f_ref[c].astype(F32) + w * f_ref[c + 1].astype(F32)
            s_ref[pl.ds(j, 48, stride=4), :] = v
        o_ref[d] = s_ref[...][:180].astype(BF)

def blend(p, f):
    V = pl.BlockSpec(memory_space=pltpu.VMEM)
    return pl.pallas_call(
        blend_kernel,
        out_shape=jax.ShapeDtypeStruct((32, 180, 128), BF),
        in_specs=[pl.BlockSpec(memory_space=pltpu.SMEM), V],
        out_specs=V,
        scratch_shapes=[pltpu.VMEM((192, 128), F32)],
        compiler_params=pltpu.CompilerParams(vmem_limit_bytes=VLIM),
    )(p, f)

def tables():
    n = np.arange(2048)[:, None]
    k = np.arange(3600)[None, :]
    f, g = [], []
    for par in range(2):
        m = np.arange(par, 1024, 2)
        ang = 2 * np.pi * ((n * m[None]) % 4096) / 4096
        f.append(np.concatenate([np.cos(ang), np.sin(ang)], 1))
        ang = 2 * np.pi * ((m[:, None] * k) % 7200) / 7200
        w = np.where(m == 0, 1.0, 2.0)[:, None] / 4096
        g.append(np.pad(np.concatenate([w * np.cos(ang), w * np.sin(ang)], 0), ((0, 0), (0, 240))))
    return np.stack(f).astype(jnp.bfloat16), np.stack(g).astype(jnp.bfloat16)

NF, NG, GC = 8, 5, 768

def dft_kernel(b_ref, f_ref, g_ref, o_ref, x_ref, sp_ref, tail_ref):
    i = pl.program_id(0)

    @pl.when(i == 0)
    def _():
        for t in range(16):
            u = b_ref[t].astype(F32)
            v = b_ref[t + 16].astype(F32)
            x_ref[0, :, t * 128:(t + 1) * 128] = (u + v).astype(BF)
            x_ref[1, :, t * 128:(t + 1) * 128] = (u - v).astype(BF)

    for s in range(NF):
        @pl.when(i == s)
        def _(s=s):
            par, blk = s // 4, s % 4
            v = jnp.dot(x_ref[par], f_ref[0], preferred_element_type=F32)
            sp_ref[par, :, blk * 256:(blk + 1) * 256] = v.astype(BF)

    for s in range(NG):
        @pl.when(i == NF + s)
        def _(s=s):
            e = jnp.dot(sp_ref[0], g_ref[0], preferred_element_type=F32)
            o = jnp.dot(sp_ref[1], g_ref[1], preferred_element_type=F32)
            first, sec = e + o, e - o
            base = s * GC
            n1 = GC if s < NG - 1 else 512
            o_ref[:, :, base:base + n1] = first[:, :n1].astype(BF).reshape(45, 4, n1)
            full = jnp.concatenate([sec, tail_ref[...]], axis=1)
            full = pltpu.roll(full, 16, axis=1)
            tail_ref[...] = sec[:, GC - 128:]
            n2 = GC if s < NG - 1 else 544
            o_ref[:, :, 3584 + base:3584 + base + n2] = full[:, :n2].astype(BF).reshape(45, 4, n2)
            if s == NG - 1:
                old = o_ref[:, :, 3584:3712]
                new = first[:, 512:640].astype(BF).reshape(45, 4, 128)
                lane = lax.broadcasted_iota(jnp.int32, (45, 4, 128), 2)
                o_ref[:, :, 3584:3712] = jnp.where(lane < 16, new, old)

def dft(b, f, g):
    V = pl.BlockSpec(memory_space=pltpu.VMEM)
    return pl.pallas_call(
        dft_kernel,
        out_shape=jax.ShapeDtypeStruct((45, 4, 7200), BF),
        grid=(NF + NG,),
        in_specs=[
            V,
            pl.BlockSpec((1, 2048, 256), lambda i: (jnp.minimum(i, NF - 1) // 4, 0, jnp.minimum(i, NF - 1) % 4)),
            pl.BlockSpec((2, 1024, GC), lambda i: (0, 0, jnp.maximum(i - NF, 0))),
        ],
        out_specs=V,
        scratch_shapes=[pltpu.VMEM((2, 180, 2048), BF), pltpu.VMEM((2, 180, 1024), BF), pltpu.VMEM((180, 128), F32)],
        compiler_params=pltpu.CompilerParams(vmem_limit_bytes=VLIM),
    )(b, f, g)

def ring(count, step):
    return [(i, (i + step) % count) for i in range(count)]


def strips_of(rows):
    pick = np.zeros((4, 128), np.float32)
    pick[[0, 1, 2, 3], [0, 1, 126, 127]] = 1.0
    return jnp.einsum("kp,crp->kcr", jnp.asarray(pick, BF), rows, preferred_element_type=F32).astype(BF)


def on_device(cells, conv_in, conv_out, blend_cycle, blend_weight):
    faces, tiles = lax.axis_size("face"), lax.axis_size("tile")
    face = lax.axis_index("face")
    me = face * tiles + lax.axis_index("tile")
    local = (blend_cycle - me * 6).astype(F32)
    params = lax.all_gather(jnp.concatenate([local, blend_weight]), "tile")
    up = lax.ppermute(cells[:, 190:, :], "face", [(i, i + 1) for i in range(faces - 1)])
    dn = lax.ppermute(cells[:, :3, :], "face", [(i + 1, i) for i in range(faces - 1)])
    strips = jnp.concatenate([strips_of(up), strips_of(cells), strips_of(dn), jnp.zeros((4, 96, 59), BF)], axis=2)
    left = lax.ppermute(strips[2:], "tile", ring(tiles, 1))
    right = lax.ppermute(strips[:2], "tile", ring(tiles, -1))
    x = regroup(cells)
    w2 = jnp.pad(conv_out, ((0, 3), (0, 0)))
    f = conv(face[None].astype(jnp.int32), conv_in, w2, x, jnp.swapaxes(up, 0, 1), jnp.swapaxes(dn, 0, 1), left, strips, right)
    b = blend(params, f)
    b = lax.all_to_all(b, "tile", split_axis=0, concat_axis=0, tiled=True)
    fwd, inv = tables()
    return dft(b, jnp.asarray(fwd), jnp.asarray(inv))


def solution(mesh):
    in_specs = (P(None, "face", "tile"), P(), P(), P(("face", "tile")), P(("face", "tile")))
    out_specs = P(None, ("face", "tile"), None)
    return jax.shard_map(on_device, mesh=mesh, in_specs=in_specs, out_specs=out_specs, check_vma=False)
```

```python
import jax
import jax.numpy as jnp
import numpy as np
from jax import lax
from jax.experimental import pallas as pl
from jax.experimental.pallas import tpu as pltpu
from jax.sharding import PartitionSpec as P

BF, F32 = jnp.bfloat16, jnp.float32
VLIM = 60 * 1024 * 1024
G = 28
NE = 7

def wide(ref):
    return jnp.concatenate([ref[t].astype(F32) for t in range(NE)], axis=1)

def rows3(v):
    n = v.shape[1]
    return jnp.concatenate([pltpu.roll(v, 4, axis=1), v, pltpu.roll(v, n - 4, axis=1)], axis=0).astype(BF)

def spread(v0, v2, dst):
    n = v0.shape[1]
    lane = lax.broadcasted_iota(jnp.int32, v0.shape, 1) % 4
    z = jnp.where(lane == 1, v0, pltpu.roll(v2, n - 2, axis=1))
    for t in range(NE):
        dst[t] = z[:, t * 128:(t + 1) * 128]

def join(p, u, o, edge):
    s = slice(u * 128, (u + 1) * 128)
    lane = lax.broadcasted_iota(jnp.int32, (o, 128), 1)
    before = jnp.where(lane == 0, edge, pltpu.roll(p[:o, s], 1, axis=1))
    after = jnp.where(lane == 127, edge, pltpu.roll(p[2 * o:, s], 127, axis=1))
    return p[o:2 * o, s] + before + after

def act(v):
    return 0.5 * v * (1.0 + jnp.tanh(0.5 * v))

def conv2_kernel(face_ref, w1_ref, w2_ref, x_ref, xh_ref, eo_ref, el_ref, er_ref, f_ref,
                 xs, h, c1, c2, sem):
    C, R = 96, x_ref.shape[0]
    face = face_ref[0]
    copies = [pltpu.make_async_copy(xh_ref.at[pl.ds(0, 2)], xs.at[pl.ds(0, 2)], sem.at[0]),
              pltpu.make_async_copy(xh_ref.at[pl.ds(2, 3)], xs.at[pl.ds(R + 2, 3)], sem.at[1]),
              pltpu.make_async_copy(x_ref, xs.at[pl.ds(2, R)], sem.at[2])]
    for c in copies:
        c.start()
    w1, w2 = w1_ref[...], w2_ref[...]
    lo = jnp.where(face == 0, 0, -1)
    hi = jnp.where(face == 3, R, R + 2)

    own, lf, rt = wide(eo_ref), wide(el_ref), wide(er_ref)
    n = NE * 128
    pos = lax.broadcasted_iota(jnp.int32, (C, n), 1)
    z = jnp.where(pos % 4 < 2, lf, rt)
    t0 = pltpu.roll(jnp.where(pos % 4 == 0, z, own), 1, axis=1)
    t2 = pltpu.roll(jnp.where(pos % 4 == 3, z, own), n - 1, axis=1)
    p = jnp.dot(w1, rows3(z), preferred_element_type=F32)
    spread(p[:C], p[2 * C:], c1)
    he = p[C:2 * C] + jnp.dot(w1[:C], rows3(t0), preferred_element_type=F32)
    he = he + jnp.dot(w1[2 * C:], rows3(t2), preferred_element_type=F32)
    row = pos // 4
    row = jnp.where(row >= NE * 32 - 2, row - NE * 32, row)
    he = jnp.where((row >= lo) & (row < hi), act(he), 0.0)
    g = jnp.dot(w2, rows3(he), preferred_element_type=F32)
    spread(g[:48], g[96:], c2)
    for c in copies:
        c.wait()

    def pick(ref, r):
        r = jnp.where(r < 0, r + NE * 32, r)
        return pltpu.roll(ref[r // 32], 127 - 4 * (r % 32), axis=1)

    def cols(ref, i):
        return jnp.concatenate([ref[pl.ds(i, 3)].reshape(3 * C, 128), ref[pl.ds(i + 1, 3)].reshape(3 * C, 128)], axis=1)

    def hid(k):
        p = jnp.dot(w1, cols(xs, k), preferred_element_type=F32)
        out = []
        for u in range(2):
            r = k + u - 1
            v = act(join(p, u, C, pick(c1, r)))
            out.append(jnp.where((r >= lo) & (r < hi), v, 0.0).astype(BF))
        return out

    def fld(r):
        q = jnp.dot(w2, cols(h, r), preferred_element_type=F32)
        return [join(q, u, 48, pick(c2, r + u - 2)).astype(BF) for u in range(2)]

    for u in range(0, G, 2):
        h[u + 2], h[u + 3] = hid(u)

    @pl.loop(1, (R + 4) // G)
    def _(i):
        f, a = [], []
        for u in range(0, G, 2):
            f += fld((i - 1) * G + u)
            a += hid(i * G + u)
        for u in range(G):
            f_ref[(i - 1) * G + u] = f[u]
            h[i * G + u + 2] = a[u]

    for u in range(R + 4 - G, R + 2, 2):
        f_ref[u], f_ref[u + 1] = fld(u)
    q = fld(R + 2)[0].astype(F32)
    f_ref[R + 2] = jnp.where(face == 3, 0.0, q).astype(BF)

def conv2(face, w1, w2, x, xh, eo, el, er):
    R = x.shape[0]
    V = pl.BlockSpec(memory_space=pltpu.VMEM)
    A = pl.BlockSpec(memory_space=pl.ANY)
    return pl.pallas_call(
        conv2_kernel,
        out_shape=jax.ShapeDtypeStruct((R + 4, 48, 128), BF),
        in_specs=[pl.BlockSpec(memory_space=pltpu.SMEM), V, V, A, A, V, V, V],
        out_specs=V,
        scratch_shapes=[pltpu.VMEM((R + 6, 96, 128), BF), pltpu.VMEM((R + 6, 96, 128), BF),
                        pltpu.VMEM((NE, 96, 128), F32), pltpu.VMEM((NE, 48, 128), F32), pltpu.SemaphoreType.DMA((3,))],
        compiler_params=pltpu.CompilerParams(vmem_limit_bytes=VLIM),
    )(face, w1, w2, x, xh, eo, el, er)

RB = 32

def regroup2_kernel(x_ref, up_ref, dn_ref, o_ref, oh_ref, e_ref):
    C = x_ref.shape[0]
    i = pl.program_id(0)
    quad = lax.broadcasted_iota(jnp.int32, (C, 128), 1) // 4

    def ends(rows, slots, acc):
        for v, q in zip(rows, slots):
            acc = jnp.where(quad == q, pltpu.roll(v.astype(F32), (4 * q + 2) % 128, axis=1), acc)
        return acc.astype(BF)

    zero = jnp.zeros((C, 128), F32)
    y = jnp.swapaxes(x_ref[...], 0, 1)
    o_ref[...] = y
    e_ref[i] = ends([y[r] for r in range(RB)], range(RB), zero)

    @pl.when(i == 0)
    def _():
        rows = [up_ref[0], up_ref[1], dn_ref[0], dn_ref[1], dn_ref[2]]
        for r in range(5):
            oh_ref[r] = rows[r]
        e_ref[NE - 1] = ends(rows, [30, 31, 0, 1, 2], zero)

def regroup2(x, up, dn):
    c, r, p = x.shape
    V = pl.BlockSpec(memory_space=pltpu.VMEM)
    return pl.pallas_call(
        regroup2_kernel,
        out_shape=[jax.ShapeDtypeStruct((r, c, p), BF), jax.ShapeDtypeStruct((5, c, p), BF), jax.ShapeDtypeStruct((NE, c, p), BF)],
        grid=(r // RB,),
        in_specs=[pl.BlockSpec((c, RB, p), lambda i: (0, i, 0)), V, V],
        out_specs=[pl.BlockSpec((RB, c, p), lambda i: (i, 0, 0)), V, V],
        compiler_params=pltpu.CompilerParams(vmem_limit_bytes=VLIM),
    )(x, up, dn)

def blend_kernel(p_ref, f_ref, o_ref, s_ref):
    D = o_ref.shape[0]
    @pl.loop(0, D)
    def _(d):
        for j in range(4):
            c = d * 6 + p_ref[d, j].astype(jnp.int32)
            w = p_ref[d, 4 + j]
            v = (1.0 - w) * f_ref[c + 2].astype(F32) + w * f_ref[c + 3].astype(F32)
            s_ref[pl.ds(j, 48, stride=4), :] = v
        o_ref[d] = s_ref[...][:180].astype(BF)

def blend(p, f):
    V = pl.BlockSpec(memory_space=pltpu.VMEM)
    return pl.pallas_call(
        blend_kernel,
        out_shape=jax.ShapeDtypeStruct((32, 180, 128), BF),
        in_specs=[pl.BlockSpec(memory_space=pltpu.SMEM), V],
        out_specs=V,
        scratch_shapes=[pltpu.VMEM((192, 128), F32)],
        compiler_params=pltpu.CompilerParams(vmem_limit_bytes=VLIM),
    )(p, f)

def tables():
    n = np.arange(2048)[:, None]
    k = np.arange(3600)[None, :]
    f, g = [], []
    for par in range(2):
        m = np.arange(par, 1024, 2)
        ang = 2 * np.pi * ((n * m[None]) % 4096) / 4096
        f.append(np.concatenate([np.cos(ang), np.sin(ang)], 1))
        ang = 2 * np.pi * ((m[:, None] * k) % 7200) / 7200
        w = np.where(m == 0, 1.0, 2.0)[:, None] / 4096
        g.append(np.pad(np.concatenate([w * np.cos(ang), w * np.sin(ang)], 0), ((0, 0), (0, 240))))
    return np.stack(f).astype(jnp.bfloat16), np.stack(g).astype(jnp.bfloat16)

NF, NG, GC = 8, 5, 768

def dft_kernel(b_ref, f_ref, g_ref, o_ref, x_ref, sp_ref, tail_ref):
    i = pl.program_id(0)

    @pl.when(i == 0)
    def _():
        for t in range(16):
            u = b_ref[t].astype(F32)
            v = b_ref[t + 16].astype(F32)
            x_ref[0, :, t * 128:(t + 1) * 128] = (u + v).astype(BF)
            x_ref[1, :, t * 128:(t + 1) * 128] = (u - v).astype(BF)

    for s in range(NF):
        @pl.when(i == s)
        def _(s=s):
            par, blk = s // 4, s % 4
            v = jnp.dot(x_ref[par], f_ref[0], preferred_element_type=F32)
            sp_ref[par, :, blk * 256:(blk + 1) * 256] = v.astype(BF)

    for s in range(NG):
        @pl.when(i == NF + s)
        def _(s=s):
            e = jnp.dot(sp_ref[0], g_ref[0], preferred_element_type=F32)
            o = jnp.dot(sp_ref[1], g_ref[1], preferred_element_type=F32)
            first, sec = e + o, e - o
            base = s * GC
            n1 = GC if s < NG - 1 else 512
            o_ref[:, :, base:base + n1] = first[:, :n1].astype(BF).reshape(45, 4, n1)
            full = jnp.concatenate([sec, tail_ref[...]], axis=1)
            full = pltpu.roll(full, 16, axis=1)
            tail_ref[...] = sec[:, GC - 128:]
            n2 = GC if s < NG - 1 else 544
            o_ref[:, :, 3584 + base:3584 + base + n2] = full[:, :n2].astype(BF).reshape(45, 4, n2)
            if s == NG - 1:
                old = o_ref[:, :, 3584:3712]
                new = first[:, 512:640].astype(BF).reshape(45, 4, 128)
                lane = lax.broadcasted_iota(jnp.int32, (45, 4, 128), 2)
                o_ref[:, :, 3584:3712] = jnp.where(lane < 16, new, old)

def dft(b, f, g):
    V = pl.BlockSpec(memory_space=pltpu.VMEM)
    return pl.pallas_call(
        dft_kernel,
        out_shape=jax.ShapeDtypeStruct((45, 4, 7200), BF),
        grid=(NF + NG,),
        in_specs=[
            V,
            pl.BlockSpec((1, 2048, 256), lambda i: (jnp.minimum(i, NF - 1) // 4, 0, jnp.minimum(i, NF - 1) % 4)),
            pl.BlockSpec((2, 1024, GC), lambda i: (0, 0, jnp.maximum(i - NF, 0))),
        ],
        out_specs=V,
        scratch_shapes=[pltpu.VMEM((2, 180, 2048), BF), pltpu.VMEM((2, 180, 1024), BF), pltpu.VMEM((180, 128), F32)],
        compiler_params=pltpu.CompilerParams(vmem_limit_bytes=VLIM),
    )(b, f, g)


def ring(count, step):
    return [(i, (i + step) % count) for i in range(count)]


def by_tap(weight, outs):
    w = weight.reshape(weight.shape[0], 3, 3, 96).transpose(2, 0, 1, 3)
    return jnp.pad(w, ((0, 0), (0, outs - weight.shape[0]), (0, 0), (0, 0))).reshape(3 * outs, 288)


def on_device(cells, conv_in, conv_out, blend_cycle, blend_weight):
    faces, tiles = lax.axis_size("face"), lax.axis_size("tile")
    face = lax.axis_index("face")
    me = face * tiles + lax.axis_index("tile")
    up = lax.ppermute(jnp.swapaxes(cells[:, 190:, :], 0, 1), "face", [(i, i + 1) for i in range(faces - 1)])
    dn = lax.ppermute(jnp.swapaxes(cells[:, :3, :], 0, 1), "face", [(i + 1, i) for i in range(faces - 1)])
    local = (blend_cycle - me * 6).astype(F32)
    mine = jnp.pad(jnp.concatenate([local, blend_weight]), (0, 120))
    params = lax.all_to_all(jnp.broadcast_to(mine, (tiles, 1, 128)), "tile", 0, 0, tiled=True).reshape(tiles, 128)
    x, xh, e = regroup2(cells, up, dn)
    el = lax.ppermute(e, "tile", ring(tiles, 1))
    er = lax.ppermute(e, "tile", ring(tiles, -1))
    f = conv2(face[None].astype(jnp.int32), by_tap(conv_in, 96), by_tap(conv_out, 48), x, xh, e, el, er)
    b = blend(params, f)
    b = lax.all_to_all(b, "tile", split_axis=0, concat_axis=0, tiled=True)
    fwd, inv = tables()
    return dft(b, jnp.asarray(fwd), jnp.asarray(inv))


def solution(mesh):
    in_specs = (P(None, "face", "tile"), P(), P(), P(("face", "tile")), P(("face", "tile")))
    out_specs = P(None, ("face", "tile"), None)
    return jax.shard_map(on_device, mesh=mesh, in_specs=in_specs, out_specs=out_specs, check_vma=False)
```

```python
import jax
import jax.numpy as jnp
import numpy as np
from jax import lax
from jax.experimental import pallas as pl
from jax.experimental.pallas import tpu as pltpu
from jax.sharding import PartitionSpec as P

BF, F32 = jnp.bfloat16, jnp.float32
G = 28
CONV_MB, REG_MB, MIX_MB, DFT_MB = 26, 16, 6, 28
NE = 7

def wide(ref):
    return jnp.concatenate([ref[t].astype(F32) for t in range(NE)], axis=1)

def rows3(v):
    n = v.shape[1]
    return jnp.concatenate([pltpu.roll(v, 4, axis=1), v, pltpu.roll(v, n - 4, axis=1)], axis=0).astype(BF)

def spread(v0, v2, dst):
    n = v0.shape[1]
    lane = lax.broadcasted_iota(jnp.int32, v0.shape, 1) % 4
    z = jnp.where(lane == 1, v0, pltpu.roll(v2, n - 2, axis=1))
    for t in range(NE):
        dst[t] = z[:, t * 128:(t + 1) * 128]

def join(p, u, o, edge):
    s = slice(u * 128, (u + 1) * 128)
    lane = lax.broadcasted_iota(jnp.int32, (o, 128), 1)
    before = jnp.where(lane == 0, edge, pltpu.roll(p[:o, s], 1, axis=1))
    after = jnp.where(lane == 127, edge, pltpu.roll(p[2 * o:, s], 127, axis=1))
    return p[o:2 * o, s] + before + after

def act(v):
    return 0.5 * v * (1.0 + jnp.tanh(0.5 * v))

def conv2_kernel(face_ref, w1_ref, w2_ref, x_hbm, eo_ref, el_ref, er_ref, f_ref, xs, h, c1, c2, sem):
    C, R = 96, x_hbm.shape[0] - 6
    N = (R + 4) // G

    def rows_in(i):
        part = pl.ds(i * G + 2, G)
        return pltpu.make_async_copy(x_hbm.at[part], xs.at[part], sem.at[i])

    head = pltpu.make_async_copy(x_hbm.at[pl.ds(0, 2)], xs.at[pl.ds(0, 2)], sem.at[N])
    head.start()
    for i in range(N):
        rows_in(i).start()
    face = face_ref[0]
    w1, w2 = w1_ref[...], w2_ref[...]
    lo = jnp.where(face == 0, 0, -1)
    hi = jnp.where(face == 3, R, R + 2)

    own, lf, rt = wide(eo_ref), wide(el_ref), wide(er_ref)
    n = NE * 128
    pos = lax.broadcasted_iota(jnp.int32, (C, n), 1)
    z = jnp.where(pos % 4 < 2, lf, rt)
    t0 = pltpu.roll(jnp.where(pos % 4 == 0, z, own), 1, axis=1)
    t2 = pltpu.roll(jnp.where(pos % 4 == 3, z, own), n - 1, axis=1)
    p = jnp.dot(w1, rows3(z), preferred_element_type=F32)
    spread(p[:C], p[2 * C:], c1)
    he = p[C:2 * C] + jnp.dot(w1[:C], rows3(t0), preferred_element_type=F32)
    he = he + jnp.dot(w1[2 * C:], rows3(t2), preferred_element_type=F32)
    row = pos // 4
    row = jnp.where(row >= NE * 32 - 2, row - NE * 32, row)
    he = jnp.where((row >= lo) & (row < hi), act(he), 0.0)
    g = jnp.dot(w2, rows3(he), preferred_element_type=F32)
    spread(g[:48], g[96:], c2)

    def pick(ref, r):
        r = jnp.where(r < 0, r + NE * 32, r)
        return pltpu.roll(ref[r // 32], 127 - 4 * (r % 32), axis=1)

    def cols(ref, i):
        return jnp.concatenate([ref[pl.ds(i, 3)].reshape(3 * C, 128), ref[pl.ds(i + 1, 3)].reshape(3 * C, 128)], axis=1)

    def hid(k):
        p = jnp.dot(w1, cols(xs, k), preferred_element_type=F32)
        out = []
        for u in range(2):
            r = k + u - 1
            v = act(join(p, u, C, pick(c1, r)))
            out.append(jnp.where((r >= lo) & (r < hi), v, 0.0).astype(BF))
        return out

    def fld(r):
        q = jnp.dot(w2, cols(h, r), preferred_element_type=F32)
        return [join(q, u, 48, pick(c2, r + u - 2)).astype(BF) for u in range(2)]

    head.wait()
    rows_in(0).wait()
    for u in range(0, G, 2):
        h[u + 2], h[u + 3] = hid(u)

    @pl.loop(1, N)
    def _(i):
        rows_in(i).wait()
        f, a = [], []
        for u in range(0, G, 2):
            f += fld((i - 1) * G + u)
            a += hid(i * G + u)
        for u in range(G):
            f_ref[(i - 1) * G + u] = f[u]
            h[i * G + u + 2] = a[u]

    for u in range(R + 4 - G, R + 2, 2):
        f_ref[u], f_ref[u + 1] = fld(u)
    q = fld(R + 2)[0].astype(F32)
    f_ref[R + 2] = jnp.where(face == 3, 0.0, q).astype(BF)


def near(x):
    return pltpu.with_memory_space_constraint(x, pltpu.VMEM)


V = pl.BlockSpec(memory_space=pltpu.VMEM)
S = pl.BlockSpec(memory_space=pltpu.SMEM)
A = pl.BlockSpec(memory_space=pltpu.HBM)


def far(x):
    return pltpu.with_memory_space_constraint(x, pltpu.HBM)


def conv2(face, w1, w2, x, eo, el, er):
    R = x.shape[0] - 6
    return pl.pallas_call(
        conv2_kernel,
        out_shape=pltpu.VMEM((R + 4, 48, 128), BF),
        in_specs=[S, V, V, A, V, V, V],
        out_specs=V,
        scratch_shapes=[pltpu.VMEM((R + 6, 96, 128), BF), pltpu.VMEM((R + 6, 96, 128), BF), pltpu.VMEM((NE, 96, 128), F32),
                        pltpu.VMEM((NE, 48, 128), F32), pltpu.SemaphoreType.DMA(((R + 4) // G + 1,))],
        compiler_params=pltpu.CompilerParams(vmem_limit_bytes=CONV_MB << 20),
    )(face, w1, w2, far(x), eo, el, er)


def blend_kernel(par_ref, f_ref, o_ref, mix):
    @pl.loop(0, o_ref.shape[0] // 4)
    def _(i):
        for t in range(4):
            d = 4 * i + t
            for j in range(4):
                c = 6 * d + par_ref[d, j].astype(jnp.int32) + 2
                w = par_ref[d, 4 + j]
                v = (1.0 - w) * f_ref[c].astype(F32) + w * f_ref[c + 1].astype(F32)
                mix[t, pl.ds(j, 48, stride=4), :] = v
        for t in range(4):
            o_ref[4 * i + t] = mix[t, :180].astype(BF)


def blend(par, f):
    return pl.pallas_call(
        blend_kernel,
        out_shape=pltpu.VMEM((par.shape[0], 180, 128), BF),
        in_specs=[S, V],
        out_specs=V,
        scratch_shapes=[pltpu.VMEM((4, 192, 128), F32)],
        compiler_params=pltpu.CompilerParams(vmem_limit_bytes=MIX_MB << 20),
    )(par, near(f))


RB = 32


def regroup_kernel(x_hbm, up_ref, dn_ref, o_hbm, e_ref, xb, ob, isem, osem):
    C, R = x_hbm.shape[:2]
    N = R // RB
    quad = lax.broadcasted_iota(jnp.int32, (C, 128), 1) // 4

    def load(i):
        return pltpu.make_async_copy(x_hbm.at[:, pl.ds(pl.multiple_of(i * RB, RB), RB), :], xb.at[i], isem.at[i])

    def store(i):
        part = pl.ds(i * RB + 2, RB)
        return pltpu.make_async_copy(ob.at[part], o_hbm.at[part], osem.at[i])

    for i in range(N):
        load(i).start()

    def ends(rows, slots):
        acc = jnp.zeros((C, 128), F32)
        for v, q in zip(rows, slots):
            acc = jnp.where(quad == q, pltpu.roll(v.astype(F32), (4 * q + 2) % 128, axis=1), acc)
        return acc.astype(BF)

    rows = [up_ref[0], up_ref[1], dn_ref[0], dn_ref[1], dn_ref[2]]
    for r, v in zip((0, 1, R + 2, R + 3, R + 4), rows):
        ob[r] = v
    ob[R + 5] = jnp.zeros_like(rows[0])
    rims = [pltpu.make_async_copy(ob.at[pl.ds(p, n)], o_hbm.at[pl.ds(p, n)], osem.at[N + t])
            for t, (p, n) in enumerate(((0, 2), (R + 2, 4)))]
    for c in rims:
        c.start()
    e_ref[NE - 1] = ends(rows, [30, 31, 0, 1, 2])

    @pl.loop(0, N)
    def _(i):
        load(i).wait()
        y = jnp.swapaxes(xb[i], 0, 1)
        ob[pl.ds(i * RB + 2, RB)] = y
        store(i).start()
        e_ref[i] = ends([y[r] for r in range(RB)], range(RB))

    for c in rims:
        c.wait()
    for i in range(N):
        store(i).wait()


def regroup(x, up, dn):
    c, r, p = x.shape
    return pl.pallas_call(
        regroup_kernel,
        out_shape=[pltpu.HBM((r + 6, c, p), BF), pltpu.VMEM((NE, c, p), BF)],
        in_specs=[A, V, V],
        out_specs=[A, V],
        scratch_shapes=[pltpu.VMEM((r // RB, c, RB, p), BF), pltpu.VMEM((r + 6, c, p), BF),
                        pltpu.SemaphoreType.DMA((r // RB,)), pltpu.SemaphoreType.DMA((r // RB + 2,))],
        compiler_params=pltpu.CompilerParams(vmem_limit_bytes=REG_MB << 20),
    )(far(x), up, dn)


def tables4():
    n = np.arange(1024)[:, None]
    k = np.arange(1800)[None, :]
    f, g = [], []
    for r in range(4):
        m = np.arange(r, 1024, 4)
        ang = 2 * np.pi * ((n * m[None]) % 4096) / 4096
        f.append(np.concatenate([np.cos(ang), np.sin(ang)], 1))
        ang = 2 * np.pi * ((m[:, None] * k) % 7200) / 7200
        w = np.where(m == 0, 1.0, 2.0)[:, None] / 4096
        g.append(np.pad(np.concatenate([w * np.cos(ang), w * np.sin(ang)], 0), ((0, 0), (0, 120))))
    return np.stack(f).astype(jnp.bfloat16), np.stack(g).astype(jnp.bfloat16)

GC = 640
M = 192

def dft4_kernel(b_ref, f_ref, g_hbm, o_hbm, x_ref, sp_ref, tail_ref, g_ref, o_ref, gsem, osem):
    loads = []
    for s in range(3):
        part = pl.ds(s * GC, GC)
        loads.append(pltpu.make_async_copy(g_hbm.at[:, :, part], g_ref.at[:, :, part], gsem.at[s]))
        loads[s].start()
    stores = []

    def send(lo, hi):
        part = pl.ds(lo, hi - lo)
        c = pltpu.make_async_copy(o_ref.at[:, :, part], o_hbm.at[:, :, part], osem.at[len(stores)])
        c.start()
        stores.append(c)

    for t in range(8):
        x0, x1, x2, x3 = [b_ref[t + 8 * a].astype(F32) for a in range(4)]
        s02, s13 = x0 + x2, x1 + x3
        c = slice(t * 128, (t + 1) * 128)
        x_ref[0, :180, c] = (s02 + s13).astype(BF)
        x_ref[1, :180, c] = (s02 - s13).astype(BF)
        x_ref[2, :180, c] = (x0 - x2).astype(BF)
        x_ref[3, :180, c] = (x1 - x3).astype(BF)

    for s, (r, parts) in enumerate(((0, (0,)), (2, (1,)), (1, (2, 3)), (3, (2, 3)))):
        if len(parts) == 1:
            v = jnp.dot(x_ref[parts[0]], f_ref[r], preferred_element_type=F32)
            sp_ref[r // 2] = v.astype(BF)
        else:
            v = jnp.dot(x_ref[2:4].reshape(2 * M, 1024), f_ref[r], preferred_element_type=F32)
            p, q = v[:M], v[M:]
            sg = 1.0 if r == 1 else -1.0
            cc = p[:, :256] - sg * q[:, 256:]
            ss = p[:, 256:] + sg * q[:, :256]
            at = 2 if r == 1 else 4
            sp_ref[at] = jnp.concatenate([cc, ss], axis=1).astype(BF)
            sp_ref[at + 1] = jnp.concatenate([ss, -cc], axis=1).astype(BF)

    for s in range(3):
        base = s * GC
        cs = slice(base, base + GC)
        loads[s].wait()
        a0 = jnp.dot(sp_ref[0], g_ref[0, :, cs], preferred_element_type=F32)
        a2 = jnp.dot(sp_ref[1], g_ref[2, :, cs], preferred_element_type=F32)
        r1 = jnp.dot(sp_ref[2:4].reshape(2 * M, 512), g_ref[1, :, cs], preferred_element_type=F32)
        r3 = jnp.dot(sp_ref[4:6].reshape(2 * M, 512), g_ref[3, :, cs], preferred_element_type=F32)
        ev, od = a0 + a2, a0 - a2
        ap, bm = r1[:M] + r3[:M], r1[M:] - r3[M:]
        base = s * GC
        lane = lax.broadcasted_iota(jnp.int32, (M, 128), 1)
        n = GC if s < 2 else 1800 - 2 * GC
        for q, v in enumerate((ev + ap, od + bm, ev - ap, od - bm)):
            v = v[:180]
            end = v[:, GC - 128:]
            sh = 8 * q
            if q:
                v = pltpu.roll(jnp.concatenate([v, tail_ref[q, :180]], axis=1), sh, axis=1)
            tail_ref[q, :180] = end
            c0 = q * 1792 + base
            if s < 2:
                o_ref[:, :, c0:c0 + GC] = v[:, :GC].astype(BF).reshape(45, 4, GC)
                send(c0 + (128 if q and not s else 0), c0 + GC)
            else:
                m = 512 + (128 if q == 3 else 0)
                m = min(m, 7200 - c0)
                o_ref[:, :, c0:c0 + m] = v[:, :m].astype(BF).reshape(45, 4, m)
                if q < 3:
                    c1 = c0 + 512
                    new = v[:, 512:640].astype(BF).reshape(45, 4, 128)
                    old = o_ref[:, :, c1:c1 + 128]
                    ln = lax.broadcasted_iota(jnp.int32, (45, 4, 128), 2)
                    o_ref[:, :, c1:c1 + 128] = jnp.where(ln < 8 * (q + 1), new, old)
                    m = 640
                send(c0, c0 + m)

    for c in stores:
        c.wait()


def dft4(b, f, g):
    return pl.pallas_call(
        dft4_kernel,
        out_shape=jax.ShapeDtypeStruct((45, 4, 7200), BF),
        in_specs=[V, V, A],
        out_specs=A,
        scratch_shapes=[pltpu.VMEM((4, M, 1024), BF), pltpu.VMEM((6, M, 512), BF), pltpu.VMEM((4, M, 128), F32),
                        pltpu.VMEM((4, 512, 3 * GC), BF), pltpu.VMEM((45, 4, 7200), BF),
                        pltpu.SemaphoreType.DMA((3,)), pltpu.SemaphoreType.DMA((12,))],
        compiler_params=pltpu.CompilerParams(vmem_limit_bytes=DFT_MB << 20),
    )(b, near(f), far(g))


def ring(count, step):
    return [(i, (i + step) % count) for i in range(count)]


def by_tap(weight, outs):
    w = weight.reshape(weight.shape[0], 3, 3, 96).transpose(2, 0, 1, 3)
    return jnp.pad(w, ((0, 0), (0, outs - weight.shape[0]), (0, 0), (0, 0))).reshape(3 * outs, 288)


def on_device(cells, conv_in, conv_out, blend_cycle, blend_weight):
    faces, tiles = lax.axis_size("face"), lax.axis_size("tile")
    face = lax.axis_index("face")
    me = face * tiles + lax.axis_index("tile")
    up = lax.ppermute(jnp.swapaxes(cells[:, 190:, :], 0, 1), "face", [(i, i + 1) for i in range(faces - 1)])
    dn = lax.ppermute(jnp.swapaxes(cells[:, :3, :], 0, 1), "face", [(i + 1, i) for i in range(faces - 1)])
    local = (blend_cycle - me * 6).astype(F32)
    mine = jnp.pad(jnp.concatenate([local, blend_weight]), (0, 120))
    params = lax.all_to_all(jnp.broadcast_to(mine, (tiles, 1, 128)), "tile", 0, 0, tiled=True).reshape(tiles, 128)
    x, e = regroup(cells, up, dn)
    el = lax.ppermute(e, "tile", ring(tiles, 1))
    er = lax.ppermute(e, "tile", ring(tiles, -1))
    f = conv2(face[None].astype(jnp.int32), by_tap(conv_in, 96), by_tap(conv_out, 48), x, e, el, er)
    b = blend(params, f)
    b = lax.all_to_all(b, "tile", split_axis=0, concat_axis=0, tiled=True)
    fwd, inv = tables4()
    return dft4(b, jnp.asarray(fwd), jnp.asarray(inv))


def solution(mesh):
    in_specs = (P(None, "face", "tile"), P(), P(), P(("face", "tile")), P(("face", "tile")))
    out_specs = P(None, ("face", "tile"), None)
    return jax.shard_map(on_device, mesh=mesh, in_specs=in_specs, out_specs=out_specs, check_vma=False)
```

```python
import jax
import jax.numpy as jnp
import numpy as np
from jax import lax
from jax.experimental import pallas as pl
from jax.experimental.pallas import tpu as pltpu
from jax.sharding import PartitionSpec as P

BF, F32 = jnp.bfloat16, jnp.float32
G = 98
CONV_MB, REG_MB, MIX_MB, DFT_MB = 40, 16, 6, 28
NE = 7

def wide(ref):
    return jnp.concatenate([ref[t] for t in range(NE)], axis=1)

def rows3(v):
    n = v.shape[1]
    return jnp.concatenate([pltpu.roll(v, 4, axis=1), v, pltpu.roll(v, n - 4, axis=1)], axis=0)

def spread(v0, v2, dst):
    n = v0.shape[1]
    lane = lax.broadcasted_iota(jnp.int32, v0.shape, 1) % 4
    z = jnp.where(lane == 1, v0, pltpu.roll(v2, n - 2, axis=1))
    for t in range(NE):
        dst[t] = z[:, t * 128:(t + 1) * 128]

def join(p, u, o, edge):
    s = slice(u * 128, (u + 1) * 128)
    lane = lax.broadcasted_iota(jnp.int32, (o, 128), 1)
    before = jnp.where(lane == 0, edge, pltpu.roll(p[:o, s], 1, axis=1))
    after = jnp.where(lane == 127, edge, pltpu.roll(p[2 * o:, s], 127, axis=1))
    return p[o:2 * o, s] + before + after

def act(v):
    return 0.5 * v * (1.0 + jnp.tanh(0.5 * v))

def conv2_kernel(face_ref, w1_ref, w2_ref, x_hbm, eo_ref, el_ref, er_ref, f_ref, xs, h, c1, c2, sem):
    C, R = 96, x_hbm.shape[0] - 6
    N = (R + 4) // G

    def rows_in(i):
        part = pl.ds(i * G + 2, G)
        return pltpu.make_async_copy(x_hbm.at[part], xs.at[part], sem.at[i])

    head = pltpu.make_async_copy(x_hbm.at[pl.ds(0, 2)], xs.at[pl.ds(0, 2)], sem.at[N])
    head.start()
    for i in range(N):
        rows_in(i).start()
    face = face_ref[0]
    w1, w2 = w1_ref[...], w2_ref[...]
    lo = jnp.where(face == 0, 0, -1)
    hi = jnp.where(face == 3, R, R + 2)

    own, lf, rt = wide(eo_ref), wide(el_ref), wide(er_ref)
    n = NE * 128
    pos = lax.broadcasted_iota(jnp.int32, (C, n), 1)
    z = jnp.where(pos % 4 < 2, lf, rt)
    t0 = pltpu.roll(jnp.where(pos % 4 == 0, z, own), 1, axis=1)
    t2 = pltpu.roll(jnp.where(pos % 4 == 3, z, own), n - 1, axis=1)
    p = jnp.dot(w1, rows3(z), preferred_element_type=F32)
    spread(p[:C], p[2 * C:], c1)

    def pick(ref, r):
        r = jnp.where(r < 0, r + NE * 32, r)
        return pltpu.roll(ref[r // 32], 127 - 4 * (r % 32), axis=1)

    def cols(ref, i):
        return jnp.concatenate([ref[pl.ds(i, 3)].reshape(3 * C, 128), ref[pl.ds(i + 1, 3)].reshape(3 * C, 128)], axis=1)

    def hid(k):
        p = jnp.dot(w1, cols(xs, k), preferred_element_type=F32)
        out = []
        for u in range(2):
            r = k + u - 1
            v = act(join(p, u, C, pick(c1, r)))
            out.append(jnp.where((r >= lo) & (r < hi), v, 0.0).astype(BF))
        return out

    def fld(r):
        q = jnp.dot(w2, cols(h, r), preferred_element_type=F32)
        return [join(q, u, 48, pick(c2, r + u - 2)).astype(BF) for u in range(2)]

    head.wait()
    rows_in(0).wait()
    he = p[C:2 * C] + jnp.dot(w1[:C], rows3(t0), preferred_element_type=F32)
    he = he + jnp.dot(w1[2 * C:], rows3(t2), preferred_element_type=F32)
    row = pos // 4
    row = jnp.where(row >= NE * 32 - 2, row - NE * 32, row)
    he = jnp.where((row >= lo) & (row < hi), act(he), 0.0).astype(BF)
    g = jnp.dot(w2, rows3(he), preferred_element_type=F32)
    spread(g[:48], g[96:], c2)
    for u in range(0, G, 2):
        h[u + 2], h[u + 3] = hid(u)

    @pl.loop(1, N)
    def _(i):
        rows_in(i).wait()
        f, a = [], []
        for u in range(0, G, 2):
            f += fld((i - 1) * G + u)
            a += hid(i * G + u)
        for u in range(G):
            f_ref[(i - 1) * G + u] = f[u]
            h[i * G + u + 2] = a[u]

    for u in range(R + 4 - G, R + 2, 2):
        f_ref[u], f_ref[u + 1] = fld(u)
    q = fld(R + 2)[0].astype(F32)
    f_ref[R + 2] = jnp.where(face == 3, 0.0, q).astype(BF)


def near(x):
    return pltpu.with_memory_space_constraint(x, pltpu.VMEM)


V = pl.BlockSpec(memory_space=pltpu.VMEM)
S = pl.BlockSpec(memory_space=pltpu.SMEM)
A = pl.BlockSpec(memory_space=pltpu.HBM)


def far(x):
    return pltpu.with_memory_space_constraint(x, pltpu.HBM)


def conv2(face, w1, w2, x, eo, el, er):
    R = x.shape[0] - 6
    return pl.pallas_call(
        conv2_kernel,
        out_shape=pltpu.VMEM((R + 4, 48, 128), BF),
        in_specs=[S, V, V, A, V, V, V],
        out_specs=V,
        scratch_shapes=[pltpu.VMEM((R + 6, 96, 128), BF), pltpu.VMEM((R + 6, 96, 128), BF), pltpu.VMEM((NE, 96, 128), F32),
                        pltpu.VMEM((NE, 48, 128), F32), pltpu.SemaphoreType.DMA(((R + 4) // G + 1,))],
        cost_estimate=pl.CostEstimate(flops=2 * 432 * 288 * 128 * (R + 4), bytes_accessed=2 * 128 * (R + 6) * 144, transcendentals=96 * 128 * (R + 4)),
        compiler_params=pltpu.CompilerParams(vmem_limit_bytes=CONV_MB << 20),
    )(face, w1, w2, far(x), eo, el, er)


def blend_kernel(par_ref, f_ref, o_ref, mix):
    @pl.loop(0, o_ref.shape[0] // 4)
    def _(i):
        for t in range(4):
            d = 4 * i + t
            for j in range(4):
                c = 6 * d + par_ref[d, j].astype(jnp.int32) + 2
                w = par_ref[d, 4 + j]
                v = (1.0 - w) * f_ref[c].astype(F32) + w * f_ref[c + 1].astype(F32)
                mix[t, pl.ds(j, 48, stride=4), :] = v
        for t in range(4):
            o_ref[4 * i + t] = mix[t, :180].astype(BF)


def blend(par, f):
    return pl.pallas_call(
        blend_kernel,
        out_shape=pltpu.VMEM((par.shape[0], 180, 128), BF),
        in_specs=[S, V],
        out_specs=V,
        scratch_shapes=[pltpu.VMEM((4, 192, 128), F32)],
        cost_estimate=pl.CostEstimate(flops=4 * 32 * 4 * 48 * 128, bytes_accessed=2 * 32 * 128 * 560, transcendentals=0),
        compiler_params=pltpu.CompilerParams(vmem_limit_bytes=MIX_MB << 20),
    )(par, near(f))


RB = 32


def regroup_kernel(x_hbm, up_ref, dn_ref, o_hbm, e_ref, xb, ob, isem, osem):
    C, R = x_hbm.shape[:2]
    N = R // RB
    quad = lax.broadcasted_iota(jnp.int32, (C, 128), 1) // 4

    def load(i):
        return pltpu.make_async_copy(x_hbm.at[:, pl.ds(pl.multiple_of(i * RB, RB), RB), :], xb.at[i], isem.at[i])

    def store(i):
        part = pl.ds(i * RB + 2, RB)
        return pltpu.make_async_copy(ob.at[part], o_hbm.at[part], osem.at[i])

    for i in range(N):
        load(i).start()

    def ends(rows, slots):
        acc = jnp.zeros((C, 128), BF)
        for v, q in zip(rows, slots):
            acc = jnp.where(quad == q, pltpu.roll(v, (4 * q + 2) % 128, axis=1), acc)
        return acc

    rows = [up_ref[0], up_ref[1], dn_ref[0], dn_ref[1], dn_ref[2]]
    for r, v in zip((0, 1, R + 2, R + 3, R + 4), rows):
        ob[r] = v
    ob[R + 5] = jnp.zeros_like(rows[0])
    rims = [pltpu.make_async_copy(ob.at[pl.ds(p, n)], o_hbm.at[pl.ds(p, n)], osem.at[N + t])
            for t, (p, n) in enumerate(((0, 2), (R + 2, 4)))]
    for c in rims:
        c.start()
    e_ref[NE - 1] = ends(rows, [30, 31, 0, 1, 2])

    @pl.loop(0, N)
    def _(i):
        load(i).wait()
        y = jnp.swapaxes(xb[i], 0, 1)
        ob[pl.ds(i * RB + 2, RB)] = y
        store(i).start()
        e_ref[i] = ends([y[r] for r in range(RB)], range(RB))

    for c in rims:
        c.wait()
    for i in range(N):
        store(i).wait()


def regroup(x, up, dn):
    c, r, p = x.shape
    return pl.pallas_call(
        regroup_kernel,
        out_shape=[pltpu.HBM((r + 6, c, p), BF), pltpu.VMEM((NE, c, p), BF)],
        in_specs=[A, V, V],
        out_specs=[A, V],
        scratch_shapes=[pltpu.VMEM((r // RB, c, RB, p), BF), pltpu.VMEM((r + 6, c, p), BF),
                        pltpu.SemaphoreType.DMA((r // RB,)), pltpu.SemaphoreType.DMA((r // RB + 2,))],
        cost_estimate=pl.CostEstimate(flops=2 * c * r * p, bytes_accessed=4 * c * r * p, transcendentals=0),
        compiler_params=pltpu.CompilerParams(vmem_limit_bytes=REG_MB << 20),
    )(far(x), up, dn)


def tables4():
    n = np.arange(1024)[:, None]
    k = np.arange(1800)[None, :]
    f, g = [], []
    for r in range(4):
        m = np.arange(r, 1024, 4)
        ang = 2 * np.pi * ((n * m[None]) % 4096) / 4096
        f.append(np.concatenate([np.cos(ang), np.sin(ang)], 1))
        ang = 2 * np.pi * ((m[:, None] * k) % 7200) / 7200
        w = np.where(m == 0, 1.0, 2.0)[:, None] / 4096
        g.append(np.pad(np.concatenate([w * np.cos(ang), w * np.sin(ang)], 0), ((0, 0), (0, 248))))
    parts = f + [v[:, c:c + GC] for c in range(0, 2048, GC) for v in g]
    t = np.concatenate(parts, 0).astype(jnp.bfloat16)
    return t[:4096], t[4096:].reshape(NG, 2048, GC)


GC = 512
NG = 4
M = 192

def dft4_kernel(b_ref, t_ref, g_hbm, o_hbm, x_ref, sp_ref, tail_ref, g_ref, o_ref, gsem, osem):
    loads = [pltpu.make_async_copy(g_hbm.at[s], g_ref.at[s], gsem.at[s]) for s in range(NG)]
    for c in loads:
        c.start()
    stores = []

    def send(lo, hi):
        part = pl.ds(lo, hi - lo)
        c = pltpu.make_async_copy(o_ref.at[:, :, part], o_hbm.at[:, :, part], osem.at[len(stores)])
        c.start()
        stores.append(c)

    for t in range(8):
        x0, x1, x2, x3 = [b_ref[t + 8 * a].astype(F32) for a in range(4)]
        s02, s13 = x0 + x2, x1 + x3
        c = slice(t * 128, (t + 1) * 128)
        x_ref[0, :180, c] = (s02 + s13).astype(BF)
        x_ref[1, :180, c] = (s02 - s13).astype(BF)
        x_ref[2, :180, c] = (x0 - x2).astype(BF)
        x_ref[3, :180, c] = (x1 - x3).astype(BF)

    for s, (r, parts) in enumerate(((0, (0,)), (2, (1,)), (1, (2, 3)), (3, (2, 3)))):
        if len(parts) == 1:
            v = jnp.dot(x_ref[parts[0]], t_ref[r * 1024:(r + 1) * 1024], preferred_element_type=F32)
            sp_ref[r // 2] = v.astype(BF)
        else:
            v = jnp.dot(x_ref[2:4].reshape(2 * M, 1024), t_ref[r * 1024:(r + 1) * 1024], preferred_element_type=F32)
            p, q = v[:M], v[M:]
            sg = 1.0 if r == 1 else -1.0
            cc = p[:, :256] - sg * q[:, 256:]
            ss = p[:, 256:] + sg * q[:, :256]
            at = 2 if r == 1 else 4
            sp_ref[at] = jnp.concatenate([cc, ss], axis=1).astype(BF)
            sp_ref[at + 1] = jnp.concatenate([ss, -cc], axis=1).astype(BF)

    def inv(r, s):
        return g_ref[s, r * 512:(r + 1) * 512, :GC if s < NG - 1 else 384]

    for s in range(NG):
        base = s * GC
        loads[s].wait()
        a0 = jnp.dot(sp_ref[0], inv(0, s), preferred_element_type=F32)
        a2 = jnp.dot(sp_ref[1], inv(2, s), preferred_element_type=F32)
        r1 = jnp.dot(sp_ref[2:4].reshape(2 * M, 512), inv(1, s), preferred_element_type=F32)
        r3 = jnp.dot(sp_ref[4:6].reshape(2 * M, 512), inv(3, s), preferred_element_type=F32)
        ev, od = a0 + a2, a0 - a2
        ap, bm = r1[:M] + r3[:M], r1[M:] - r3[M:]
        for q, v in enumerate((ev + ap, od + bm, ev - ap, od - bm)):
            v = v[:180]
            end = v[:, v.shape[1] - 128:]
            sh = 8 * q
            if q:
                v = pltpu.roll(jnp.concatenate([v, tail_ref[q, :180]], axis=1), sh, axis=1)
            tail_ref[q, :180] = end
            c0 = q * 1792 + base
            if s < NG - 1:
                o_ref[:, :, c0:c0 + GC] = v[:, :GC].astype(BF).reshape(45, 4, GC)
                send(c0 + (128 if q and not s else 0), c0 + GC)
            else:
                m = 256 if q < 3 else 7200 - c0
                o_ref[:, :, c0:c0 + m] = v[:, :m].astype(BF).reshape(45, 4, m)
                if q < 3:
                    c1 = c0 + 256
                    new = v[:, 256:384].astype(BF).reshape(45, 4, 128)
                    old = o_ref[:, :, c1:c1 + 128]
                    ln = lax.broadcasted_iota(jnp.int32, (45, 4, 128), 2)
                    o_ref[:, :, c1:c1 + 128] = jnp.where(ln < 8 * (q + 1), new, old)
                    m = 384
                send(c0, c0 + m)

    for c in stores:
        c.wait()


def dft4(b, t, g):
    return pl.pallas_call(
        dft4_kernel,
        out_shape=jax.ShapeDtypeStruct((45, 4, 7200), BF),
        in_specs=[V, V, A],
        out_specs=A,
        scratch_shapes=[pltpu.VMEM((4, M, 1024), BF), pltpu.VMEM((6, M, 512), BF), pltpu.VMEM((4, M, 128), F32),
                        pltpu.VMEM((NG, 2048, GC), BF), pltpu.VMEM((45, 4, 7200), BF),
                        pltpu.SemaphoreType.DMA((NG,)), pltpu.SemaphoreType.DMA((4 * NG,))],
        compiler_params=pltpu.CompilerParams(vmem_limit_bytes=DFT_MB << 20),
    )(b, near(t), far(g))


def ring(count, step):
    return [(i, (i + step) % count) for i in range(count)]


def by_tap(weight, outs):
    w = weight.reshape(weight.shape[0], 3, 3, 96).transpose(2, 0, 1, 3)
    return jnp.pad(w, ((0, 0), (0, outs - weight.shape[0]), (0, 0), (0, 0))).reshape(3 * outs, 288)


def on_device(cells, conv_in, conv_out, blend_cycle, blend_weight):
    faces, tiles = lax.axis_size("face"), lax.axis_size("tile")
    face = lax.axis_index("face")
    me = face * tiles + lax.axis_index("tile")
    up = lax.ppermute(jnp.swapaxes(cells[:, 190:, :], 0, 1), "face", [(i, i + 1) for i in range(faces - 1)])
    dn = lax.ppermute(jnp.swapaxes(cells[:, :3, :], 0, 1), "face", [(i + 1, i) for i in range(faces - 1)])
    local = (blend_cycle - me * 6).astype(F32)
    mine = jnp.pad(jnp.concatenate([local, blend_weight]), (0, 120))
    params = lax.all_to_all(jnp.broadcast_to(mine, (tiles, 1, 128)), "tile", 0, 0, tiled=True).reshape(tiles, 128)
    x, e = regroup(cells, up, dn)
    el = lax.ppermute(e, "tile", ring(tiles, 1))
    er = lax.ppermute(e, "tile", ring(tiles, -1))
    f = conv2(face[None].astype(jnp.int32), by_tap(conv_in, 96), by_tap(conv_out, 48), x, e, el, er)
    b = blend(params, f)
    b = lax.all_to_all(b, "tile", split_axis=0, concat_axis=0, tiled=True)
    fwd, inv = tables4()
    return dft4(b, jnp.asarray(fwd), jnp.asarray(inv))


def solution(mesh):
    in_specs = (P(None, "face", "tile"), P(), P(), P(("face", "tile")), P(("face", "tile")))
    out_specs = P(None, ("face", "tile"), None)
    return jax.shard_map(on_device, mesh=mesh, in_specs=in_specs, out_specs=out_specs, check_vma=False)
```

```python
import jax
import jax.numpy as jnp
import numpy as np
from jax import lax
from jax.experimental import pallas as pl
from jax.experimental.pallas import tpu as pltpu
from jax.sharding import PartitionSpec as P

BF, F32 = jnp.bfloat16, jnp.float32
G = 98
CONV_MB, REG_MB, MIX_MB, DFT_MB = 40, 16, 6, 28
NE = 7

def wide(ref):
    return jnp.concatenate([ref[t] for t in range(NE)], axis=1)

def rows3(v):
    n = v.shape[1]
    return jnp.concatenate([pltpu.roll(v, 4, axis=1), v, pltpu.roll(v, n - 4, axis=1)], axis=0)

def spread(v0, v2, dst):
    n = v0.shape[1]
    lane = lax.broadcasted_iota(jnp.int32, v0.shape, 1) % 4
    z = jnp.where(lane == 1, v0, pltpu.roll(v2, n - 2, axis=1))
    for t in range(NE):
        dst[t] = z[:, t * 128:(t + 1) * 128]

def join(p, u, o, edge):
    s = slice(u * 128, (u + 1) * 128)
    lane = lax.broadcasted_iota(jnp.int32, (o, 128), 1)
    before = jnp.where(lane == 0, edge, pltpu.roll(p[:o, s], 1, axis=1))
    after = jnp.where(lane == 127, edge, pltpu.roll(p[2 * o:, s], 127, axis=1))
    return p[o:2 * o, s] + before + after

def act(v):
    return 0.5 * v * (1.0 + jnp.tanh(0.5 * v))

def conv2_kernel(face_ref, w1_ref, w2_ref, x_hbm, eo_ref, el_ref, er_ref, f_ref, xs, h, c1, c2, wa, wb, sem):
    C, R = 96, x_hbm.shape[0] - 6
    N = (R + 4) // G

    def rows_in(i):
        part = pl.ds(i * G + 2, G)
        return pltpu.make_async_copy(x_hbm.at[part], xs.at[part], sem.at[i])

    head = pltpu.make_async_copy(x_hbm.at[pl.ds(0, 2)], xs.at[pl.ds(0, 2)], sem.at[N])
    head.start()
    for i in range(N):
        rows_in(i).start()
    face = face_ref[0]
    for a in range(3):
        for b in range(3):
            tap = slice((3 * a + b) * C, (3 * a + b + 1) * C)
            wa[b * C:(b + 1) * C, a * C:(a + 1) * C] = w1_ref[:, tap]
            wb[b * 48:(b + 1) * 48, a * C:(a + 1) * C] = w2_ref[:, tap]
    w1, w2 = wa[...], wb[...]
    lo = jnp.where(face == 0, 0, -1)
    hi = jnp.where(face == 3, R, R + 2)

    own, lf, rt = wide(eo_ref), wide(el_ref), wide(er_ref)
    n = NE * 128
    pos = lax.broadcasted_iota(jnp.int32, (C, n), 1)
    z = jnp.where(pos % 4 < 2, lf, rt)
    t0 = pltpu.roll(jnp.where(pos % 4 == 0, z, own), 1, axis=1)
    t2 = pltpu.roll(jnp.where(pos % 4 == 3, z, own), n - 1, axis=1)
    p = jnp.dot(w1, rows3(z), preferred_element_type=F32)
    spread(p[:C], p[2 * C:], c1)

    def pick(ref, r):
        r = jnp.where(r < 0, r + NE * 32, r)
        return pltpu.roll(ref[r // 32], 127 - 4 * (r % 32), axis=1)

    def cols(ref, i):
        return jnp.concatenate([ref[pl.ds(i, 3)].reshape(3 * C, 128), ref[pl.ds(i + 1, 3)].reshape(3 * C, 128)], axis=1)

    def hid(k):
        p = jnp.dot(w1, cols(xs, k), preferred_element_type=F32)
        out = []
        for u in range(2):
            r = k + u - 1
            v = act(join(p, u, C, pick(c1, r)))
            out.append(jnp.where((r >= lo) & (r < hi), v, 0.0).astype(BF))
        return out

    def fld(r):
        q = jnp.dot(w2, cols(h, r), preferred_element_type=F32)
        return [join(q, u, 48, pick(c2, r + u - 2)).astype(BF) for u in range(2)]

    head.wait()
    rows_in(0).wait()
    he = p[C:2 * C] + jnp.dot(w1[:C], rows3(t0), preferred_element_type=F32)
    he = he + jnp.dot(w1[2 * C:], rows3(t2), preferred_element_type=F32)
    row = pos // 4
    row = jnp.where(row >= NE * 32 - 2, row - NE * 32, row)
    he = jnp.where((row >= lo) & (row < hi), act(he), 0.0).astype(BF)
    g = jnp.dot(w2, rows3(he), preferred_element_type=F32)
    spread(g[:48], g[96:], c2)
    for u in range(0, G, 2):
        h[u + 2], h[u + 3] = hid(u)

    @pl.loop(1, N)
    def _(i):
        rows_in(i).wait()
        f, a = [], []
        for u in range(0, G, 2):
            f += fld((i - 1) * G + u)
            a += hid(i * G + u)
        for u in range(G):
            f_ref[(i - 1) * G + u] = f[u]
            h[i * G + u + 2] = a[u]

    for u in range(R + 4 - G, R + 2, 2):
        f_ref[u], f_ref[u + 1] = fld(u)
    q = fld(R + 2)[0].astype(F32)
    f_ref[R + 2] = jnp.where(face == 3, 0.0, q).astype(BF)


def near(x):
    return pltpu.with_memory_space_constraint(x, pltpu.VMEM)


V = pl.BlockSpec(memory_space=pltpu.VMEM)
S = pl.BlockSpec(memory_space=pltpu.SMEM)
A = pl.BlockSpec(memory_space=pltpu.HBM)


def far(x):
    return pltpu.with_memory_space_constraint(x, pltpu.HBM)


def conv2(face, w1, w2, x, eo, el, er):
    R = x.shape[0] - 6
    return pl.pallas_call(
        conv2_kernel,
        out_shape=pltpu.VMEM((R + 4, 48, 128), BF),
        in_specs=[S, V, V, A, V, V, V],
        out_specs=V,
        scratch_shapes=[pltpu.VMEM((R + 6, 96, 128), BF), pltpu.VMEM((R + 6, 96, 128), BF), pltpu.VMEM((NE, 96, 128), F32),
                        pltpu.VMEM((NE, 48, 128), F32), pltpu.VMEM((288, 288), BF), pltpu.VMEM((144, 288), BF),
                        pltpu.SemaphoreType.DMA(((R + 4) // G + 1,))],
        cost_estimate=pl.CostEstimate(flops=2 * 432 * 288 * 128 * (R + 4), bytes_accessed=2 * 128 * (R + 6) * 144, transcendentals=96 * 128 * (R + 4)),
        compiler_params=pltpu.CompilerParams(vmem_limit_bytes=CONV_MB << 20),
    )(face, w1, w2, far(x), eo, el, er)


def blend_kernel(par_ref, f_ref, o_ref, mix):
    @pl.loop(0, o_ref.shape[0] // 4)
    def _(i):
        for t in range(4):
            d = 4 * i + t
            for j in range(4):
                c = 6 * d + par_ref[d, j].astype(jnp.int32) + 2
                w = par_ref[d, 4 + j]
                v = (1.0 - w) * f_ref[c].astype(F32) + w * f_ref[c + 1].astype(F32)
                mix[t, pl.ds(j, 48, stride=4), :] = v
        for t in range(4):
            o_ref[4 * i + t] = mix[t, :180].astype(BF)


def blend(par, f):
    return pl.pallas_call(
        blend_kernel,
        out_shape=pltpu.VMEM((par.shape[0], 180, 128), BF),
        in_specs=[S, V],
        out_specs=V,
        scratch_shapes=[pltpu.VMEM((4, 192, 128), F32)],
        cost_estimate=pl.CostEstimate(flops=4 * 32 * 4 * 48 * 128, bytes_accessed=2 * 32 * 128 * 560, transcendentals=0),
        compiler_params=pltpu.CompilerParams(vmem_limit_bytes=MIX_MB << 20),
    )(par, near(f))


RB = 32


def regroup_kernel(x_hbm, up_ref, dn_ref, o_hbm, e_ref, xb, ob, isem, osem):
    C, R = x_hbm.shape[:2]
    N = R // RB
    quad = lax.broadcasted_iota(jnp.int32, (C, 128), 1) // 4

    def load(i):
        return pltpu.make_async_copy(x_hbm.at[:, pl.ds(pl.multiple_of(i * RB, RB), RB), :], xb.at[i], isem.at[i])

    def store(i):
        part = pl.ds(i * RB + 2, RB)
        return pltpu.make_async_copy(ob.at[part], o_hbm.at[part], osem.at[i])

    for i in range(N):
        load(i).start()

    def ends(rows, slots):
        acc = jnp.zeros((C, 128), BF)
        for v, q in zip(rows, slots):
            acc = jnp.where(quad == q, pltpu.roll(v, (4 * q + 2) % 128, axis=1), acc)
        return acc

    rows = [up_ref[0], up_ref[1], dn_ref[0], dn_ref[1], dn_ref[2]]
    for r, v in zip((0, 1, R + 2, R + 3, R + 4), rows):
        ob[r] = v
    ob[R + 5] = jnp.zeros_like(rows[0])
    rims = [pltpu.make_async_copy(ob.at[pl.ds(p, n)], o_hbm.at[pl.ds(p, n)], osem.at[N + t])
            for t, (p, n) in enumerate(((0, 2), (R + 2, 4)))]
    for c in rims:
        c.start()
    e_ref[NE - 1] = ends(rows, [30, 31, 0, 1, 2])

    @pl.loop(0, N)
    def _(i):
        load(i).wait()
        y = jnp.swapaxes(xb[i], 0, 1)
        ob[pl.ds(i * RB + 2, RB)] = y
        store(i).start()
        e_ref[i] = ends([y[r] for r in range(RB)], range(RB))

    for c in rims:
        c.wait()
    for i in range(N):
        store(i).wait()


def regroup(x, up, dn):
    c, r, p = x.shape
    return pl.pallas_call(
        regroup_kernel,
        out_shape=[pltpu.HBM((r + 6, c, p), BF), pltpu.VMEM((NE, c, p), BF)],
        in_specs=[A, V, V],
        out_specs=[A, V],
        scratch_shapes=[pltpu.VMEM((r // RB, c, RB, p), BF), pltpu.VMEM((r + 6, c, p), BF),
                        pltpu.SemaphoreType.DMA((r // RB,)), pltpu.SemaphoreType.DMA((r // RB + 2,))],
        cost_estimate=pl.CostEstimate(flops=2 * c * r * p, bytes_accessed=4 * c * r * p, transcendentals=0),
        compiler_params=pltpu.CompilerParams(vmem_limit_bytes=REG_MB << 20),
    )(far(x), up, dn)


def tables4():
    n = np.arange(1024)[:, None]
    k = np.arange(1800)[None, :]
    f, g = [], []
    for r in range(4):
        m = np.arange(r, 1024, 4)
        ang = 2 * np.pi * ((n * m[None]) % 4096) / 4096
        f.append(np.concatenate([np.cos(ang), np.sin(ang)], 1))
        ang = 2 * np.pi * ((m[:, None] * k) % 7200) / 7200
        w = np.where(m == 0, 1.0, 2.0)[:, None] / 4096
        g.append(np.pad(np.concatenate([w * np.cos(ang), w * np.sin(ang)], 0), ((0, 0), (0, 248))))
    parts = f + [v[:, c:c + GC] for c in range(0, 2048, GC) for v in g]
    t = np.concatenate(parts, 0).astype(jnp.bfloat16)
    return t[:4096], t[4096:].reshape(NG, 2048, GC)


GC = 512
NG = 4
M = 192

def dft4_kernel(b_ref, t_ref, g_hbm, o_hbm, x_ref, sp_ref, tail_ref, g_ref, o_ref, gsem, osem):
    loads = [pltpu.make_async_copy(g_hbm.at[s], g_ref.at[s], gsem.at[s]) for s in range(NG)]
    for c in loads:
        c.start()
    stores = []

    def send(lo, hi):
        part = pl.ds(lo, hi - lo)
        c = pltpu.make_async_copy(o_ref.at[:, :, part], o_hbm.at[:, :, part], osem.at[len(stores)])
        c.start()
        stores.append(c)

    for t in range(8):
        x0, x1, x2, x3 = [b_ref[t + 8 * a].astype(F32) for a in range(4)]
        s02, s13 = x0 + x2, x1 + x3
        c = slice(t * 128, (t + 1) * 128)
        x_ref[0, :180, c] = (s02 + s13).astype(BF)
        x_ref[1, :180, c] = (s02 - s13).astype(BF)
        x_ref[2, :180, c] = (x0 - x2).astype(BF)
        x_ref[3, :180, c] = (x1 - x3).astype(BF)

    for s, (r, parts) in enumerate(((0, (0,)), (2, (1,)), (1, (2, 3)), (3, (2, 3)))):
        if len(parts) == 1:
            v = jnp.dot(x_ref[parts[0]], t_ref[r * 1024:(r + 1) * 1024], preferred_element_type=F32)
            sp_ref[r // 2] = v.astype(BF)
        else:
            v = jnp.dot(x_ref[2:4].reshape(2 * M, 1024), t_ref[r * 1024:(r + 1) * 1024], preferred_element_type=F32)
            p, q = v[:M], v[M:]
            sg = 1.0 if r == 1 else -1.0
            cc = p[:, :256] - sg * q[:, 256:]
            ss = p[:, 256:] + sg * q[:, :256]
            at = 2 if r == 1 else 4
            sp_ref[at] = jnp.concatenate([cc, ss], axis=1).astype(BF)
            sp_ref[at + 1] = jnp.concatenate([ss, -cc], axis=1).astype(BF)

    def inv(r, s):
        return g_ref[s, r * 512:(r + 1) * 512, :GC if s < NG - 1 else 384]

    for s in range(NG):
        base = s * GC
        loads[s].wait()
        a0 = jnp.dot(sp_ref[0], inv(0, s), preferred_element_type=F32)
        a2 = jnp.dot(sp_ref[1], inv(2, s), preferred_element_type=F32)
        r1 = jnp.dot(sp_ref[2:4].reshape(2 * M, 512), inv(1, s), preferred_element_type=F32)
        r3 = jnp.dot(sp_ref[4:6].reshape(2 * M, 512), inv(3, s), preferred_element_type=F32)
        ev, od = a0 + a2, a0 - a2
        ap, bm = r1[:M] + r3[:M], r1[M:] - r3[M:]
        for q, v in enumerate((ev + ap, od + bm, ev - ap, od - bm)):
            v = v[:180]
            end = v[:, v.shape[1] - 128:]
            sh = 8 * q
            if q:
                v = pltpu.roll(jnp.concatenate([v, tail_ref[q, :180]], axis=1), sh, axis=1)
            tail_ref[q, :180] = end
            c0 = q * 1792 + base
            if s < NG - 1:
                o_ref[:, :, c0:c0 + GC] = v[:, :GC].astype(BF).reshape(45, 4, GC)
                send(c0 + (128 if q and not s else 0), c0 + GC)
            else:
                m = 256 if q < 3 else 7200 - c0
                o_ref[:, :, c0:c0 + m] = v[:, :m].astype(BF).reshape(45, 4, m)
                if q < 3:
                    c1 = c0 + 256
                    new = v[:, 256:384].astype(BF).reshape(45, 4, 128)
                    old = o_ref[:, :, c1:c1 + 128]
                    ln = lax.broadcasted_iota(jnp.int32, (45, 4, 128), 2)
                    o_ref[:, :, c1:c1 + 128] = jnp.where(ln < 8 * (q + 1), new, old)
                    m = 384
                send(c0, c0 + m)

    for c in stores:
        c.wait()


def dft4(b, t, g):
    return pl.pallas_call(
        dft4_kernel,
        out_shape=jax.ShapeDtypeStruct((45, 4, 7200), BF),
        in_specs=[V, V, A],
        out_specs=A,
        scratch_shapes=[pltpu.VMEM((4, M, 1024), BF), pltpu.VMEM((6, M, 512), BF), pltpu.VMEM((4, M, 128), F32),
                        pltpu.VMEM((NG, 2048, GC), BF), pltpu.VMEM((45, 4, 7200), BF),
                        pltpu.SemaphoreType.DMA((NG,)), pltpu.SemaphoreType.DMA((4 * NG,))],
        compiler_params=pltpu.CompilerParams(vmem_limit_bytes=DFT_MB << 20),
    )(b, near(t), far(g))


def ring(count, step):
    return [(i, (i + step) % count) for i in range(count)]


def on_device(cells, conv_in, conv_out, blend_cycle, blend_weight):
    faces, tiles = lax.axis_size("face"), lax.axis_size("tile")
    face = lax.axis_index("face")
    me = face * tiles + lax.axis_index("tile")
    up = lax.ppermute(jnp.swapaxes(cells[:, 190:, :], 0, 1), "face", [(i, i + 1) for i in range(faces - 1)])
    dn = lax.ppermute(jnp.swapaxes(cells[:, :3, :], 0, 1), "face", [(i + 1, i) for i in range(faces - 1)])
    local = (blend_cycle - me * 6).astype(F32)
    mine = jnp.pad(jnp.concatenate([local, blend_weight]), (0, 120))
    params = lax.all_to_all(jnp.broadcast_to(mine, (tiles, 1, 128)), "tile", 0, 0, tiled=True).reshape(tiles, 128)
    x, e = regroup(cells, up, dn)
    el = lax.ppermute(e, "tile", ring(tiles, 1))
    er = lax.ppermute(e, "tile", ring(tiles, -1))
    f = conv2(face[None].astype(jnp.int32), conv_in, jnp.pad(conv_out, ((0, 3), (0, 0))), x, e, el, er)
    b = blend(params, f)
    b = lax.all_to_all(b, "tile", split_axis=0, concat_axis=0, tiled=True)
    fwd, inv = tables4()
    return dft4(b, jnp.asarray(fwd), jnp.asarray(inv))


def solution(mesh):
    in_specs = (P(None, "face", "tile"), P(), P(), P(("face", "tile")), P(("face", "tile")))
    out_specs = P(None, ("face", "tile"), None)
    return jax.shard_map(on_device, mesh=mesh, in_specs=in_specs, out_specs=out_specs, check_vma=False)
```

```python
import jax
import jax.numpy as jnp
import numpy as np
from jax import lax
from jax.experimental import pallas as pl
from jax.experimental.pallas import tpu as pltpu
from jax.sharding import PartitionSpec as P

BF, F32 = jnp.bfloat16, jnp.float32
G = 98
CONV_MB, REG_MB, MIX_MB, DFT_MB = 40, 16, 6, 24
NE = 7

def wide(ref):
    return jnp.concatenate([ref[t] for t in range(NE)], axis=1)

def rows3(v):
    n = v.shape[1]
    return jnp.concatenate([pltpu.roll(v, 4, axis=1), v, pltpu.roll(v, n - 4, axis=1)], axis=0)

def spread(v0, v2, dst):
    n = v0.shape[1]
    lane = lax.broadcasted_iota(jnp.int32, v0.shape, 1) % 4
    z = jnp.where(lane == 1, v0, pltpu.roll(v2, n - 2, axis=1))
    for t in range(NE):
        dst[t] = z[:, t * 128:(t + 1) * 128]

def join(p, u, o, edge):
    s = slice(u * 128, (u + 1) * 128)
    lane = lax.broadcasted_iota(jnp.int32, (o, 128), 1)
    before = jnp.where(lane == 0, edge, pltpu.roll(p[:o, s], 1, axis=1))
    after = jnp.where(lane == 127, edge, pltpu.roll(p[2 * o:, s], 127, axis=1))
    return p[o:2 * o, s] + before + after

def act(v):
    return 0.5 * v * (1.0 + jnp.tanh(0.5 * v))

def conv2_kernel(face_ref, w1_ref, w2_ref, x_hbm, eo_ref, el_ref, er_ref, f_ref, xs, h, c1, c2, wa, wb, sem):
    C, R = 96, x_hbm.shape[0] - 6
    N = (R + 4) // G

    def rows_in(i):
        part = pl.ds(i * G + 2, G)
        return pltpu.make_async_copy(x_hbm.at[part], xs.at[part], sem.at[i])

    head = pltpu.make_async_copy(x_hbm.at[pl.ds(0, 2)], xs.at[pl.ds(0, 2)], sem.at[N])
    head.start()
    for i in range(N):
        rows_in(i).start()
    face = face_ref[0]
    for a in range(3):
        for b in range(3):
            tap = slice((3 * a + b) * C, (3 * a + b + 1) * C)
            wa[b * C:(b + 1) * C, a * C:(a + 1) * C] = w1_ref[:, tap]
            wb[b * 48:(b + 1) * 48, a * C:(a + 1) * C] = w2_ref[:, tap]
    w1, w2 = wa[...], wb[...]
    lo = jnp.where(face == 0, 0, -1)
    hi = jnp.where(face == 3, R, R + 2)

    own, lf, rt = wide(eo_ref), wide(el_ref), wide(er_ref)
    n = NE * 128
    pos = lax.broadcasted_iota(jnp.int32, (C, n), 1)
    z = jnp.where(pos % 4 < 2, lf, rt)
    t0 = pltpu.roll(jnp.where(pos % 4 == 0, z, own), 1, axis=1)
    t2 = pltpu.roll(jnp.where(pos % 4 == 3, z, own), n - 1, axis=1)
    p = jnp.dot(w1, rows3(z), preferred_element_type=F32)
    spread(p[:C], p[2 * C:], c1)

    def pick(ref, r):
        r = jnp.where(r < 0, r + NE * 32, r)
        return pltpu.roll(ref[r // 32], 127 - 4 * (r % 32), axis=1)

    def cols(ref, i):
        return jnp.concatenate([ref[pl.ds(i, 3)].reshape(3 * C, 128), ref[pl.ds(i + 1, 3)].reshape(3 * C, 128)], axis=1)

    def hid(k):
        p = jnp.dot(w1, cols(xs, k), preferred_element_type=F32)
        out = []
        for u in range(2):
            r = k + u - 1
            v = act(join(p, u, C, pick(c1, r)))
            out.append(jnp.where((r >= lo) & (r < hi), v, 0.0).astype(BF))
        return out

    def fld(r):
        q = jnp.dot(w2, cols(h, r), preferred_element_type=F32)
        return [join(q, u, 48, pick(c2, r + u - 2)).astype(BF) for u in range(2)]

    head.wait()
    rows_in(0).wait()
    he = p[C:2 * C] + jnp.dot(w1[:C], rows3(t0), preferred_element_type=F32)
    he = he + jnp.dot(w1[2 * C:], rows3(t2), preferred_element_type=F32)
    row = pos // 4
    row = jnp.where(row >= NE * 32 - 2, row - NE * 32, row)
    he = jnp.where((row >= lo) & (row < hi), act(he), 0.0).astype(BF)
    g = jnp.dot(w2, rows3(he), preferred_element_type=F32)
    spread(g[:48], g[96:], c2)
    for u in range(0, G, 2):
        h[u + 2], h[u + 3] = hid(u)

    @pl.loop(1, N)
    def _(i):
        rows_in(i).wait()
        f, a = [], []
        for u in range(0, G, 2):
            f += fld((i - 1) * G + u)
            a += hid(i * G + u)
        for u in range(G):
            f_ref[(i - 1) * G + u] = f[u]
            h[i * G + u + 2] = a[u]

    for u in range(R + 4 - G, R + 2, 2):
        f_ref[u], f_ref[u + 1] = fld(u)
    q = fld(R + 2)[0].astype(F32)
    f_ref[R + 2] = jnp.where(face == 3, 0.0, q).astype(BF)


def near(x):
    return pltpu.with_memory_space_constraint(x, pltpu.VMEM)


V = pl.BlockSpec(memory_space=pltpu.VMEM)
S = pl.BlockSpec(memory_space=pltpu.SMEM)
A = pl.BlockSpec(memory_space=pltpu.HBM)


def far(x):
    return pltpu.with_memory_space_constraint(x, pltpu.HBM)


def conv2(face, w1, w2, x, eo, el, er):
    R = x.shape[0] - 6
    return pl.pallas_call(
        conv2_kernel,
        out_shape=pltpu.VMEM((R + 4, 48, 128), BF),
        in_specs=[S, V, V, A, V, V, V],
        out_specs=V,
        scratch_shapes=[pltpu.VMEM((R + 6, 96, 128), BF), pltpu.VMEM((R + 6, 96, 128), BF), pltpu.VMEM((NE, 96, 128), F32),
                        pltpu.VMEM((NE, 48, 128), F32), pltpu.VMEM((288, 288), BF), pltpu.VMEM((144, 288), BF),
                        pltpu.SemaphoreType.DMA(((R + 4) // G + 1,))],
        cost_estimate=pl.CostEstimate(flops=2 * 432 * 288 * 128 * (R + 4), bytes_accessed=2 * 128 * (R + 6) * 144, transcendentals=96 * 128 * (R + 4)),
        compiler_params=pltpu.CompilerParams(vmem_limit_bytes=CONV_MB << 20),
    )(face, w1, w2, far(x), eo, el, er)


def blend_kernel(par_ref, f_ref, o_ref, mix):
    @pl.loop(0, o_ref.shape[0] // 4)
    def _(i):
        for t in range(4):
            d = 4 * i + t
            for j in range(4):
                c = 6 * d + par_ref[d, j].astype(jnp.int32) + 2
                w = par_ref[d, 4 + j]
                v = (1.0 - w) * f_ref[c].astype(F32) + w * f_ref[c + 1].astype(F32)
                mix[t, pl.ds(j, 48, stride=4), :] = v
        for t in range(4):
            o_ref[4 * i + t] = mix[t, :180].astype(BF)


def blend(par, f):
    return pl.pallas_call(
        blend_kernel,
        out_shape=pltpu.VMEM((par.shape[0], 180, 128), BF),
        in_specs=[S, V],
        out_specs=V,
        scratch_shapes=[pltpu.VMEM((4, 192, 128), F32)],
        cost_estimate=pl.CostEstimate(flops=4 * 32 * 4 * 48 * 128, bytes_accessed=2 * 32 * 128 * 560, transcendentals=0),
        compiler_params=pltpu.CompilerParams(vmem_limit_bytes=MIX_MB << 20),
    )(par, near(f))


RB = 32


def regroup_kernel(x_hbm, up_ref, dn_ref, o_hbm, e_ref, xb, ob, isem, osem):
    C, R = x_hbm.shape[:2]
    N = R // RB
    quad = lax.broadcasted_iota(jnp.int32, (C, 128), 1) // 4

    def load(i):
        return pltpu.make_async_copy(x_hbm.at[:, pl.ds(pl.multiple_of(i * RB, RB), RB), :], xb.at[i], isem.at[i])

    def store(i):
        part = pl.ds(i * RB + 2, RB)
        return pltpu.make_async_copy(ob.at[part], o_hbm.at[part], osem.at[i])

    for i in range(N):
        load(i).start()

    def ends(rows, slots):
        acc = jnp.zeros((C, 128), BF)
        for v, q in zip(rows, slots):
            acc = jnp.where(quad == q, pltpu.roll(v, (4 * q + 2) % 128, axis=1), acc)
        return acc

    rows = [up_ref[0], up_ref[1], dn_ref[0], dn_ref[1], dn_ref[2]]
    for r, v in zip((0, 1, R + 2, R + 3, R + 4), rows):
        ob[r] = v
    ob[R + 5] = jnp.zeros_like(rows[0])
    rims = [pltpu.make_async_copy(ob.at[pl.ds(p, n)], o_hbm.at[pl.ds(p, n)], osem.at[N + t])
            for t, (p, n) in enumerate(((0, 2), (R + 2, 4)))]
    for c in rims:
        c.start()
    e_ref[NE - 1] = ends(rows, [30, 31, 0, 1, 2])

    @pl.loop(0, N)
    def _(i):
        load(i).wait()
        y = jnp.swapaxes(xb[i], 0, 1)
        ob[pl.ds(i * RB + 2, RB)] = y
        store(i).start()
        e_ref[i] = ends([y[r] for r in range(RB)], range(RB))

    for c in rims:
        c.wait()
    for i in range(N):
        store(i).wait()


def regroup(x, up, dn):
    c, r, p = x.shape
    return pl.pallas_call(
        regroup_kernel,
        out_shape=[pltpu.HBM((r + 6, c, p), BF), pltpu.VMEM((NE, c, p), BF)],
        in_specs=[A, V, V],
        out_specs=[A, V],
        scratch_shapes=[pltpu.VMEM((r // RB, c, RB, p), BF), pltpu.VMEM((r + 6, c, p), BF),
                        pltpu.SemaphoreType.DMA((r // RB,)), pltpu.SemaphoreType.DMA((r // RB + 2,))],
        cost_estimate=pl.CostEstimate(flops=2 * c * r * p, bytes_accessed=4 * c * r * p, transcendentals=0),
        compiler_params=pltpu.CompilerParams(vmem_limit_bytes=REG_MB << 20),
    )(far(x), up, dn)


GC, NG, M = 512, 4, 192


def tables4():
    k = np.arange(256)
    n, x = np.arange(1024), np.arange(1920)
    af = 2 * np.pi * ((n[:, None] * k[None]) % 1024) / 1024
    ag = 2 * np.pi * ((4 * k[:, None] * x[None]) % 7200) / 7200
    f = np.concatenate([np.cos(af), np.sin(af)], 1)
    g = np.concatenate([np.cos(ag), np.sin(ag)], 0) * 2 / 4096

    def turns(pos, period):
        rows = []
        for r in (1, 2, 3):
            a = 2 * np.pi * (r * pos) / period
            rows += [np.cos(a), np.sin(a)]
        return np.stack(rows + [0 * pos, 0 * pos]).astype(np.float32)

    g = np.pad(g, ((0, 0), (0, NG * GC - 1920)))
    t = np.concatenate([f] + [g[:, s * GC:(s + 1) * GC] for s in range(NG)], 0)
    return t.astype(jnp.bfloat16), turns(n, 4096), turns(x, 7200)


def dft4_kernel(b_ref, t_ref, tf_ref, tg_ref, o_hbm, x_ref, sp_ref, tail_ref, o_ref, osem):
    stores = []

    def send(lo, hi):
        part = pl.ds(lo, hi - lo)
        c = pltpu.make_async_copy(o_ref.at[:, :, part], o_hbm.at[:, :, part], osem.at[len(stores)])
        c.start()
        stores.append(c)

    for t in range(8):
        x0, x1, x2, x3 = [b_ref[t + 8 * a].astype(F32) for a in range(4)]
        s02, s13, p, q = x0 + x2, x1 + x3, x0 - x2, x1 - x3
        y2 = s02 - s13
        c = slice(t * 128, (t + 1) * 128)
        c1, s1, c2, s2, c3, s3 = [tf_ref[i:i + 1, c] for i in range(6)]
        parts = (s02 + s13, p * c1 - q * s1, -(p * s1 + q * c1), y2 * c2, -(y2 * s2), p * c3 + q * s3, q * c3 - p * s3)
        for i, v in enumerate(parts):
            x_ref[i, :180, c] = v.astype(BF)

    v = jnp.dot(x_ref[0], t_ref[:1024], preferred_element_type=F32)
    lane = lax.broadcasted_iota(jnp.int32, (M, 512), 1)
    sp_ref[0] = jnp.where(lane == 0, 0.5 * v, v).astype(BF)
    for i in (1, 3, 5):
        v = jnp.dot(x_ref[i:i + 2].reshape(2 * M, 1024), t_ref[:1024], preferred_element_type=F32)
        re, im = v[:M], v[M:]
        cc = re[:, :256] + im[:, 256:]
        ss = re[:, 256:] - im[:, :256]
        sp_ref[i] = jnp.concatenate([cc, ss], axis=1).astype(BF)
        sp_ref[i + 1] = jnp.concatenate([ss, -cc], axis=1).astype(BF)

    for s in range(NG):
        base = s * GC
        cs = slice(base, min(base + GC, 1920))
        p0, p1, q1, p2, q2, p3, q3 = [jnp.dot(sp_ref[i], t_ref[1024 + s * 512:1536 + s * 512, :cs.stop - base], preferred_element_type=F32)[:180] for i in range(7)]
        c1, s1, c2, s2, c3, s3 = [tg_ref[i:i + 1, cs] for i in range(6)]
        a2 = p2 * c2 + q2 * s2
        ap = (p1 * c1 + q1 * s1) + (p3 * c3 + q3 * s3)
        bm = (q1 * c1 - p1 * s1) - (q3 * c3 - p3 * s3)
        ev, od = p0 + a2, p0 - a2
        for q, v in enumerate((ev + ap, od + bm, ev - ap, od - bm)):
            end = v[:, v.shape[1] - 128:]
            if q:
                v = pltpu.roll(jnp.concatenate([v, tail_ref[q, :180]], axis=1), 8 * q, axis=1)
            tail_ref[q, :180] = end
            c0 = q * 1792 + base
            if s < NG - 1:
                o_ref[:, :, c0:c0 + GC] = v[:, :GC].astype(BF).reshape(45, 4, GC)
                send(c0 + (128 if q and not s else 0), c0 + GC)
            else:
                m = 256 if q < 3 else 7200 - c0
                o_ref[:, :, c0:c0 + m] = v[:, :m].astype(BF).reshape(45, 4, m)
                if q < 3:
                    n1 = c0 + 256
                    new = v[:, 256:384].astype(BF).reshape(45, 4, 128)
                    old = o_ref[:, :, n1:n1 + 128]
                    ln = lax.broadcasted_iota(jnp.int32, (45, 4, 128), 2)
                    o_ref[:, :, n1:n1 + 128] = jnp.where(ln < 8 * (q + 1), new, old)
                    m = 384
                send(c0, c0 + m)

    for c in stores:
        c.wait()


def dft4(b, t, tf, tg):
    return pl.pallas_call(
        dft4_kernel,
        out_shape=jax.ShapeDtypeStruct((45, 4, 7200), BF),
        in_specs=[V] * 4,
        out_specs=A,
        scratch_shapes=[pltpu.VMEM((7, M, 1024), BF), pltpu.VMEM((7, M, 512), BF), pltpu.VMEM((4, M, 128), F32),
                        pltpu.VMEM((45, 4, 7200), BF), pltpu.SemaphoreType.DMA((4 * NG,))],
        compiler_params=pltpu.CompilerParams(vmem_limit_bytes=DFT_MB << 20),
    )(b, near(t), tf, tg)


def ring(count, step):
    return [(i, (i + step) % count) for i in range(count)]


def on_device(cells, conv_in, conv_out, blend_cycle, blend_weight):
    faces, tiles = lax.axis_size("face"), lax.axis_size("tile")
    face = lax.axis_index("face")
    me = face * tiles + lax.axis_index("tile")
    up = lax.ppermute(jnp.swapaxes(cells[:, 190:, :], 0, 1), "face", [(i, i + 1) for i in range(faces - 1)])
    dn = lax.ppermute(jnp.swapaxes(cells[:, :3, :], 0, 1), "face", [(i + 1, i) for i in range(faces - 1)])
    local = (blend_cycle - me * 6).astype(F32)
    mine = jnp.pad(jnp.concatenate([local, blend_weight]), (0, 120))
    params = lax.all_to_all(jnp.broadcast_to(mine, (tiles, 1, 128)), "tile", 0, 0, tiled=True).reshape(tiles, 128)
    x, e = regroup(cells, up, dn)
    el = lax.ppermute(e, "tile", ring(tiles, 1))
    er = lax.ppermute(e, "tile", ring(tiles, -1))
    f = conv2(face[None].astype(jnp.int32), conv_in, jnp.pad(conv_out, ((0, 3), (0, 0))), x, e, el, er)
    b = blend(params, f)
    b = lax.all_to_all(b, "tile", split_axis=0, concat_axis=0, tiled=True)
    return dft4(b, *[jnp.asarray(t) for t in tables4()])


def solution(mesh):
    in_specs = (P(None, "face", "tile"), P(), P(), P(("face", "tile")), P(("face", "tile")))
    out_specs = P(None, ("face", "tile"), None)
    return jax.shard_map(on_device, mesh=mesh, in_specs=in_specs, out_specs=out_specs, check_vma=False)
```
